128 devices in a mesh: shard: 32 (over z, y, core), grp: 4 (over x).
Axes of the slice: x: 4, y: 4, z: 4, core: 2. Of those that a mesh axis runs over, the one named last changes fastest.
Arguments:
- embeddings: bfloat16 [98304, 1024], P(('shard', 'grp'))
- worker: int32 [98304], P(('shard', 'grp')), may hold values from 0 to 127, as said below
- label: int32 [98304], P(('shard', 'grp')), may hold values from 0 to 1, as said below
Outputs:
- nearest_similarity: float32 [98304], P(('shard', 'grp'))
The draws below stay inside these ranges and needn't reach their ends.
Inputs may be any that keep to these rules, and one draw needn't show every extreme that they name: Among the rows of one device at most 12 name the same worker; some workers are named by exactly 12 rows of every device. Among the rows of one device at most 6 name the same worker and label. Rows with equal worker and label form one cluster of at most 768 rows; some cluster holds exactly 768.
All inputs are finite; a program needn't handle non-finite values.
Results may differ from the reference program's by a relative error of at most 0.00054.
Values may be sent and summed in bfloat16 or wider, within the bound.
No kernel may reach another device: no remote copies, remote signals or barrier semaphores. Data moves between devices by JAX's collectives and lax.ppermute only.
A program may use at most 64 MiB of HBM per device.

```python
import math
import jax
import jax.numpy as jnp
from jax import lax

D = 1024
ROWS_DEV = 768
SUB = 2
MOST = 12
CLUSTER_MOST = 768
ROWS = 98304
DEVICES = 128


def slot_plan(key):
    choose_key, score_key, shuffle_key, keep_key = jax.random.split(key, 4)
    total_slots = 2 * ROWS_DEV
    loaded_count = max(DEVICES // 8, 1)
    sparse_count = max(DEVICES // 16, 2)
    worker_rank = jax.random.permutation(choose_key, DEVICES)
    loaded_worker = worker_rank < loaded_count
    sparse_worker = (worker_rank >= loaded_count) & (worker_rank < loaded_count + sparse_count)
    slot_ids = jnp.arange(total_slots, dtype=jnp.int32)
    worker_for_slot = slot_ids // MOST
    offset = slot_ids % MOST
    keep_device = jax.random.randint(keep_key, (DEVICES, 3), 0, DEVICES)
    device_ids = jnp.arange(DEVICES, dtype=jnp.int32)[:, None]
    kept = (offset[None, :] == 0) & (device_ids == keep_device[worker_for_slot, 0][None, :])
    kept = kept | (offset[None, :] == 1) & (device_ids == keep_device[worker_for_slot, 1][None, :])
    kept = kept | (offset[None, :] == 3) & (device_ids == keep_device[worker_for_slot, 2][None, :])
    sparse_slot = sparse_worker[worker_for_slot][None, :]
    kept = kept & sparse_slot
    extra_score = jnp.where(loaded_worker[worker_for_slot], 2 ** 29, 0).astype(jnp.int32)
    rank_order = jax.random.randint(score_key, (DEVICES, total_slots), 0, 2 ** 16) * total_slots
    rank_order = rank_order + slot_ids[None, :] + extra_score[None, :]
    rank_order = jnp.where(sparse_slot, jnp.broadcast_to(slot_ids[None, :], (DEVICES, total_slots)), rank_order)
    rank_order = jnp.where(kept, 2 ** 30 + slot_ids[None, :], rank_order).astype(jnp.int32)
    _, chosen = lax.top_k(rank_order, ROWS_DEV)
    shuffle = jax.random.randint(shuffle_key, (DEVICES, ROWS_DEV), 0, 2 ** 16) * ROWS_DEV
    shuffle = shuffle + jnp.arange(ROWS_DEV, dtype=jnp.int32)[None, :]
    row_order = jnp.argsort(shuffle, axis=1)
    chosen = jnp.take_along_axis(chosen, row_order, axis=1)
    return (chosen.reshape(-1).astype(jnp.int32), sparse_worker)


def draw_worker(key, part):
    plan, _ = slot_plan(key)
    return (plan // MOST).astype(jnp.int32)


def draw_label(key, part):
    plan, _ = slot_plan(key)
    return (plan % SUB).astype(jnp.int32)


def draw_embeddings(key, part):
    plan, sparse_worker = slot_plan(key)
    cluster = plan // MOST * SUB + plan % SUB
    row_sparse = sparse_worker[plan // MOST]
    sign = jnp.where(row_sparse & (plan % MOST == 3), -1.0, 1.0).astype(jnp.float32)
    key = jax.random.fold_in(key, 7)
    centre_key, strength_key, spread_key = jax.random.split(key, 3)
    centroids = jax.random.normal(centre_key, (DEVICES * SUB, D), jnp.float32)
    strength = jnp.exp(jax.random.uniform(strength_key, (DEVICES * SUB,), jnp.float32, math.log(0.4), math.log(1.5)))
    row_strength = jnp.where(row_sparse, 3.0, strength[cluster]) * sign
    spread = jax.random.normal(spread_key, (ROWS, D), jnp.float32)
    return (row_strength[:, None] * centroids[cluster] + spread).astype(jnp.bfloat16)


def setup_inputs(seed: int = 0) -> dict:
    keys = jax.random.split(jax.random.key(seed), 4)
    embeddings = draw_embeddings(jax.random.fold_in(keys[3], 71), 0)
    worker = draw_worker(jax.random.fold_in(keys[3], 71), 0)
    label = draw_label(jax.random.fold_in(keys[3], 71), 0)
    return {"embeddings": embeddings, "worker": worker, "label": label}


def reference(embeddings, worker, label):
    values = embeddings.astype(jnp.float32)
    unit = (values * lax.rsqrt(lax.optimization_barrier(jnp.sum(values * values, axis=1, keepdims=True)) + 1e-06)).astype(jnp.bfloat16)
    cluster = (worker * SUB + label).astype(jnp.int32)
    row_order = jnp.argsort(cluster, stable=True).astype(jnp.int32)
    sorted_ids = cluster[row_order]
    padded_unit = jnp.concatenate([unit[row_order], jnp.zeros((CLUSTER_MOST, D), jnp.bfloat16)], axis=0)
    padded_ids = jnp.concatenate([sorted_ids, jnp.full((CLUSTER_MOST,), -1, jnp.int32)], axis=0)
    cluster_count = DEVICES * SUB
    first_rows = jnp.searchsorted(sorted_ids, jnp.arange(cluster_count, dtype=jnp.int32)).astype(jnp.int32)
    diagonal = jnp.eye(CLUSTER_MOST, dtype=bool)

    def one_cluster(running, cluster_id):
        first_row = first_rows[cluster_id]
        block = lax.dynamic_slice_in_dim(padded_unit, first_row, CLUSTER_MOST, 0)
        block_ids = lax.dynamic_slice_in_dim(padded_ids, first_row, CLUSTER_MOST, 0)
        scores = jnp.dot(block, block.T, preferred_element_type=jnp.float32)
        inside = block_ids == cluster_id
        same = inside[:, None] & inside[None, :] & jnp.logical_not(diagonal)
        best_score = lax.optimization_barrier(jnp.max(jnp.where(same, scores, -4.0), axis=1))
        best_score = jnp.where(jnp.any(same, axis=1), best_score, -1.0)
        previous = lax.dynamic_slice_in_dim(running, first_row, CLUSTER_MOST, 0)
        running = lax.dynamic_update_slice_in_dim(running, jnp.where(inside, best_score, previous), first_row, 0)
        return (running, None)
    running = jnp.full((ROWS + CLUSTER_MOST,), -1.0, jnp.float32)
    running, _ = lax.scan(one_cluster, running, jnp.arange(cluster_count, dtype=jnp.int32))
    return jnp.zeros((ROWS,), jnp.float32).at[row_order].set(running[:ROWS])
```

```python
import jax
import jax.numpy as jnp
from jax import lax
from jax.experimental import pallas as pl
from jax.experimental.pallas import tpu as pltpu
from jax.sharding import PartitionSpec as P

SUB = 2
AXES = ("shard", "grp")
PER_LABEL = 6
WHOLE = 4
BLOCK = 256
MARK = 2.0
BF16 = jnp.bfloat16
F32 = jnp.float32


def one_hot(flags):
    return jnp.where(flags, 1.0, 0.0).astype(BF16)


def dot(a, b):
    return jnp.dot(a, b, preferred_element_type=F32)


def iota(shape, dim):
    return lax.broadcasted_iota(jnp.int32, shape, dim)


def pack_kernel(worker_ref, label_ref, emb_ref, out_ref, slot_ref):
    rows, width = emb_ref.shape
    half = width // 2
    devices = out_ref.shape[0] // 8
    clusters = devices * SUB
    worker = worker_ref[...]
    label = label_ref[...]
    cluster = worker * SUB + label

    member = iota((clusters, rows), 0) == cluster
    member_hot = one_hot(member)
    before = one_hot(iota((rows, rows), 0) < iota((rows, rows), 1))
    earlier = dot(member_hot, before)
    rank = jnp.sum(jnp.where(member, earlier, 0.0), axis=0, keepdims=True).astype(jnp.int32)
    slot_ref[...] = label * PER_LABEL + rank
    first = worker * 8 + label * 4
    whole_row = jnp.where(rank < WHOLE, first + rank, -1)
    half_row = jnp.where(rank < WHOLE, -2, first + (rank - WHOLE) * 2)
    total = dot(member_hot, jnp.ones((rows, 128), BF16)).astype(BF16)

    values = emb_ref[...].astype(F32)
    unit = (values * lax.rsqrt(jnp.sum(values * values, axis=1, keepdims=True) + 1e-06)).astype(BF16)
    left, right = unit[:, :half], unit[:, half:]

    spread = one_hot(iota((BLOCK, BLOCK // 4), 0) // 4 == iota((BLOCK, BLOCK // 4), 1))
    lane = iota((BLOCK, 128), 1)
    place = iota((BLOCK, 128), 0) % 4
    for block in range(devices * 8 // BLOCK):
        at = pl.ds(block * BLOCK, BLOCK)
        here = iota((BLOCK, rows), 0) + block * BLOCK
        count = dot(spread, total[block * BLOCK // 4 : (block + 1) * BLOCK // 4])
        held = dot(one_hot(here == whole_row), unit)
        empty = jnp.where((lane == 0) & (count <= place.astype(F32)), MARK, 0.0)
        out_ref[at, :128] = (held[:, :128] + empty).astype(BF16)
        out_ref[at, 128:width] = held[:, 128:].astype(BF16)
        held = dot(one_hot(here == half_row), left) + dot(one_hot(here == half_row + 1), right)
        empty = (lane == 0) & (place % 2 == 0) & (count <= (WHOLE + place // 2).astype(F32))
        empty = jnp.where(empty, MARK, 0.0)
        out_ref[at, width : width + 128] = (held[:, :128] + empty).astype(BF16)
        out_ref[at, width + 128 :] = held[:, 128:].astype(BF16)


def score_kernel(in_ref, best_ref, members):
    rows = in_ref.shape[0]
    devices = rows // 8
    width = members.shape[2]
    half = width // 2
    per_block = BLOCK // 8
    r, c = iota((BLOCK, BLOCK), 0), iota((BLOCK, BLOCK), 1)
    regroup = one_hot(c == r % per_block * 8 + r // per_block)
    for block in range(rows // BLOCK):
        at = pl.ds(block * BLOCK, BLOCK)
        whole = dot(regroup, in_ref[at, :width]).astype(BF16)
        halves = dot(regroup, in_ref[at, width:]).astype(BF16)
        for sub in range(8):
            lab, j = sub // 4, sub % 4
            piece = slice(sub * per_block, (sub + 1) * per_block)
            members[lab, pl.ds(j * devices + block * per_block, per_block), :] = whole[piece]
            to = pl.ds((WHOLE + j // 2) * devices + block * per_block, per_block)
            members[lab, to, pl.ds(j % 2 * half, half)] = halves[piece]
    count = members.shape[1]
    eye = jnp.where(iota((BLOCK, BLOCK), 0) == iota((BLOCK, BLOCK), 1), -8.0, 0.0)
    found = []
    for lab in range(SUB):
        everyone = members[lab]
        best = jnp.full((1, count), -8.0, F32)
        for block in range(count // BLOCK):
            at = slice(block * BLOCK, (block + 1) * BLOCK)
            mine = everyone[at]
            scores = lax.dot_general(
                mine, everyone, (((1,), (1,)), ((), ())), preferred_element_type=F32
            )
            absent = jnp.where(mine[:, :1].astype(F32) > 1.5, -8.0, 0.0)
            scores = scores + absent
            parts = []
            for other in range(count // BLOCK):
                part = scores[:, other * BLOCK : (other + 1) * BLOCK]
                if other == block:
                    part = part + eye
                parts.append(jnp.max(part, axis=0, keepdims=True))
            best = jnp.maximum(best, jnp.concatenate(parts, axis=1))
        best = jnp.where(best < -2.0, -1.0, best)
        found += [best[:, j * devices : (j + 1) * devices] for j in range(PER_LABEL)]
    found.append(jnp.zeros((128 - SUB * PER_LABEL, devices), F32))
    best_ref[...] = jnp.concatenate(found, axis=0).T


def unpack_kernel(worker_ref, slot_ref, back_ref, out_ref):
    rows = worker_ref.shape[1]
    back = back_ref[...]
    devices = back.shape[0]
    back = back.T[:16]
    high = back.astype(BF16)
    rest = back - high.astype(F32)
    middle = rest.astype(BF16)
    low = (rest - middle.astype(F32)).astype(BF16)
    chosen = one_hot(iota((devices, rows), 0) == worker_ref[...])
    values = dot(high, chosen) + dot(middle, chosen) + dot(low, chosen)
    mine = iota((16, rows), 0) == slot_ref[...]
    out_ref[...] = jnp.sum(jnp.where(mine, values, 0.0), axis=0, keepdims=True)


VMEM = pl.BlockSpec(memory_space=pltpu.VMEM)


def local(embeddings, worker, label):
    rows, width = embeddings.shape
    devices = lax.axis_size("shard") * lax.axis_size("grp")
    params = pltpu.CompilerParams(vmem_limit_bytes=40 * 2**20)
    worker = worker.reshape(1, rows)
    label = label.reshape(1, rows)
    outgoing, slot = pl.pallas_call(
        pack_kernel,
        out_shape=(
            jax.ShapeDtypeStruct((devices * 8, width * 3 // 2), BF16),
            jax.ShapeDtypeStruct((1, rows), jnp.int32),
        ),
        in_specs=[VMEM] * 3,
        out_specs=(VMEM, VMEM),
        compiler_params=params,
        name="pack",
    )(worker, label, embeddings)
    incoming = lax.all_to_all(
        outgoing.reshape(devices, 8, width * 3 // 2), AXES, split_axis=0, concat_axis=0, tiled=True
    )
    best = pl.pallas_call(
        score_kernel,
        out_shape=jax.ShapeDtypeStruct((devices, 128), F32),
        in_specs=[VMEM],
        out_specs=VMEM,
        scratch_shapes=[pltpu.VMEM((SUB, devices * PER_LABEL, width), BF16)],
        compiler_params=params,
        name="score",
    )(incoming.reshape(devices * 8, width * 3 // 2))
    returned = lax.all_to_all(
        best.reshape(devices, 1, 128), AXES, split_axis=0, concat_axis=0, tiled=True
    )
    nearest = pl.pallas_call(
        unpack_kernel,
        out_shape=jax.ShapeDtypeStruct((1, rows), F32),
        in_specs=[VMEM] * 3,
        out_specs=VMEM,
        compiler_params=params,
        name="unpack",
    )(worker, slot, returned.reshape(devices, 128))
    return nearest.reshape(rows)


def solution(mesh):
    return jax.shard_map(
        local,
        mesh=mesh,
        in_specs=(P(AXES, None), P(AXES), P(AXES)),
        out_specs=P(AXES),
        check_vma=False,
    )
```

```python
import functools

import jax
import jax.numpy as jnp
from jax import lax
from jax.experimental import pallas as pl
from jax.experimental.pallas import tpu as pltpu
from jax.sharding import PartitionSpec as P

SUB = 2
AXES = ("shard", "grp")
PER_LABEL = 6
WHOLE = 4
LATE = 2
BLOCK = 256
MARK = 2.0
BF16 = jnp.bfloat16
F32 = jnp.float32


def one_hot(flags):
    return jnp.where(flags, 1.0, 0.0).astype(BF16)


def dot(a, b):
    return jnp.dot(a, b, preferred_element_type=F32)


def dot_rows(a, b):
    return lax.dot_general(a, b, (((1,), (1,)), ((), ())), preferred_element_type=F32)


def iota(shape, dim):
    return lax.broadcasted_iota(jnp.int32, shape, dim)


def pack_kernel(worker_hbm, label_hbm, emb_hbm, out_ref, place_ref, worker_ref, label_ref, emb, late, arrived):
    rows, width = emb.shape
    half = width // 2
    clusters = out_ref.shape[0] // 4
    fetches = [
        pltpu.make_async_copy(worker_hbm, worker_ref, arrived.at[0]),
        pltpu.make_async_copy(label_hbm, label_ref, arrived.at[1]),
        pltpu.make_async_copy(emb_hbm, emb, arrived.at[2]),
    ]
    for fetch in fetches:
        fetch.start()
    before = one_hot(iota((rows, rows), 0) < iota((rows, rows), 1))
    fetches[0].wait()
    fetches[1].wait()
    worker = worker_ref[...].reshape(1, rows)
    label = label_ref[...].reshape(1, rows)
    cluster = worker * SUB + label

    member = iota((clusters, rows), 0) == cluster
    member_hot = one_hot(member)
    earlier = dot(member_hot, before)
    rank = jnp.sum(jnp.where(member, earlier, 0.0), axis=0, keepdims=True).astype(jnp.int32)
    place_ref[...] = worker * 16 + label * PER_LABEL + rank
    whole_row = jnp.where(rank < WHOLE, cluster * WHOLE + rank, -1)
    late_row = jnp.where(rank < WHOLE, -1, cluster * LATE + rank - WHOLE)
    total = dot(member_hot, jnp.ones((rows, 128), BF16)).astype(BF16)
    line = iota((BLOCK, rows), 0).astype(F32).astype(BF16)
    fetches[2].wait()

    def placed(block, target, per_cluster, first_slot, to):
        at = pl.ds(block * BLOCK, BLOCK)
        count = BLOCK // per_cluster
        inside = target - block * BLOCK
        inside = jnp.where((inside >= 0) & (inside < BLOCK), inside, -1).astype(F32).astype(BF16)
        chosen = jnp.where(line == inside, jnp.ones((), BF16), jnp.zeros((), BF16))
        values = dot(chosen, emb[...])
        values = values * lax.rsqrt(jnp.sum(values * values, axis=1, keepdims=True) + 1e-06)
        spread = one_hot(iota((BLOCK, count), 0) // per_cluster == iota((BLOCK, count), 1))
        filled = dot(spread, total[block * count : (block + 1) * count])
        slot = iota((BLOCK, 128), 0) % per_cluster + first_slot
        empty = (iota((BLOCK, 128), 1) == 0) & (filled <= slot.astype(F32))
        to[at, :128] = (values[:, :128] + jnp.where(empty, MARK, 0.0)).astype(BF16)
        to[at, 128:width] = values[:, 128:].astype(BF16)

    for block in range(clusters * LATE // BLOCK):
        placed(block, late_row, LATE, WHOLE, late)
    for block in range(clusters * WHOLE // BLOCK):
        placed(block, whole_row, WHOLE, 0, out_ref)
    r, c = iota((BLOCK, BLOCK), 0), iota((BLOCK, BLOCK), 1)
    split = one_hot(c == r % 2 * (BLOCK // 2) + r // 2)
    for block in range(clusters * LATE * 2 // BLOCK):
        source = pl.ds(block * (BLOCK // 2), BLOCK // 2)
        halves = jnp.concatenate([late[source, :half], late[source, half:]], axis=0)
        out_ref[pl.ds(block * BLOCK, BLOCK), width:] = dot(split, halves).astype(BF16)


def score_kernel(in_ref, out_ref, members):
    rows = in_ref.shape[0]
    devices = rows // 8
    count, width = members.shape[1:]
    half = width // 2
    per_block = BLOCK // 8
    r, c = iota((BLOCK, BLOCK), 0), iota((BLOCK, BLOCK), 1)
    regroup = one_hot(c == r % per_block * 8 + r // per_block)
    itself = jnp.where(r == c, -8.0, 0.0)
    for block in range(rows // BLOCK):
        at = pl.ds(block * BLOCK, BLOCK)
        whole = dot(regroup, in_ref[at, :width]).astype(BF16)
        halves = dot(regroup, in_ref[at, width:]).astype(BF16)
        for sub in range(8):
            lab, j = sub // 4, sub % 4
            piece = slice(sub * per_block, (sub + 1) * per_block)
            members[lab, pl.ds(j * devices + block * per_block, per_block), :] = whole[piece]
            to = pl.ds((WHOLE + j // 2) * devices + block * per_block, per_block)
            members[lab, to, pl.ds(j % 2 * half, half)] = halves[piece]

    blocks = count // BLOCK
    found = []
    for lab in range(SUB):
        parts = [members[lab, pl.ds(i * BLOCK, BLOCK), :] for i in range(blocks)]
        absent = [jnp.where(p[:, :128].astype(F32) > MARK - 0.5, -8.0, 0.0)[:, :1] for p in parts]
        absent_row = [jnp.broadcast_to(a, (BLOCK, 128)).T[:1] for a in absent]
        down, along = [[] for _ in parts], [[] for _ in parts]
        for i in range(blocks):
            for j in range(i, blocks):
                scores = dot_rows(parts[i], parts[j]) + absent[i]
                if i == j:
                    down[j].append(scores + itself)
                else:
                    down[j].append(scores)
                    scores = scores + absent_row[j]
                    along[i] += [scores[:, k : k + 128] for k in range(0, BLOCK, 128)]
        for i in range(blocks):
            best = jnp.max(functools.reduce(jnp.maximum, down[i]), axis=0, keepdims=True)
            if along[i]:
                other = functools.reduce(jnp.maximum, along[i]).T
                best = jnp.maximum(best, jnp.max(other, axis=0, keepdims=True))
            best = jnp.where(best < -2.0, -1.0, best)
            found += [best[:, k : k + devices] for k in range(0, BLOCK, devices)]
    found.append(jnp.zeros((128 - SUB * PER_LABEL, devices), F32))
    out_ref[...] = jnp.concatenate(found, axis=0).T


def unpack_kernel(place_ref, back_ref, out_ref):
    place = place_ref[...]
    rows = place.shape[1]
    back = back_ref[...]
    devices = back.shape[0]
    back = back.T[:16]
    high = back.astype(BF16)
    rest = back - high.astype(F32)
    middle = rest.astype(BF16)
    low = (rest - middle.astype(F32)).astype(BF16)
    chosen = one_hot(iota((devices, rows), 0) == place // 16)
    values = dot(high, chosen) + dot(middle, chosen) + dot(low, chosen)
    mine = iota((16, rows), 0) == place % 16
    out_ref[...] = jnp.sum(jnp.where(mine, values, 0.0), axis=0)


VMEM = pl.BlockSpec(memory_space=pltpu.VMEM)
HBM = pl.BlockSpec(memory_space=pltpu.HBM)
PARAMS = pltpu.CompilerParams(vmem_limit_bytes=40 * 2**20)


def exchange(array):
    return lax.all_to_all(array, AXES, split_axis=0, concat_axis=0, tiled=True)


def local(embeddings, worker, label):
    rows, width = embeddings.shape
    devices = lax.axis_size("shard") * lax.axis_size("grp")
    shape = jax.ShapeDtypeStruct
    packed = (devices * 8, width * 3 // 2)
    in_hbm = [pltpu.with_memory_space_constraint(x, pltpu.HBM) for x in (worker, label, embeddings)]
    outgoing, place = pl.pallas_call(
        pack_kernel,
        out_shape=(shape(packed, BF16), shape((1, rows), jnp.int32)),
        in_specs=[HBM] * 3,
        out_specs=(VMEM, VMEM),
        scratch_shapes=[
            pltpu.VMEM((rows,), jnp.int32),
            pltpu.VMEM((rows,), jnp.int32),
            pltpu.VMEM((rows, width), BF16),
            pltpu.VMEM((devices * SUB * LATE, width), BF16),
            pltpu.SemaphoreType.DMA((3,)),
        ],
        compiler_params=PARAMS,
        name="pack",
    )(*in_hbm)
    incoming = exchange(outgoing.reshape(devices, 8, packed[1])).reshape(packed)
    found = pl.pallas_call(
        score_kernel,
        out_shape=shape((devices, 128), F32),
        in_specs=[VMEM],
        out_specs=VMEM,
        scratch_shapes=[pltpu.VMEM((SUB, devices * PER_LABEL, width), BF16)],
        compiler_params=PARAMS,
        name="score",
    )(incoming)
    returned = exchange(found.reshape(devices, 1, 128)).reshape(devices, 128)
    return pl.pallas_call(
        unpack_kernel,
        out_shape=shape((rows,), F32),
        in_specs=[VMEM] * 2,
        out_specs=VMEM,
        compiler_params=PARAMS,
        name="unpack",
    )(place, returned)


def solution(mesh):
    return jax.shard_map(
        local,
        mesh=mesh,
        in_specs=(P(AXES, None), P(AXES), P(AXES)),
        out_specs=P(AXES),
        check_vma=False,
    )
```

```python
import functools

import jax
import jax.numpy as jnp
from jax import lax
from jax.experimental import pallas as pl
from jax.experimental.pallas import tpu as pltpu
from jax.sharding import PartitionSpec as P

SUB = 2
AXES = ("shard", "grp")
PER_LABEL = 6
WHOLE = 4
LATE = 2
BLOCK = 256
MARK = 2.0
BF16 = jnp.bfloat16
F32 = jnp.float32


def one_hot(flags):
    return jnp.where(flags, 1.0, 0.0).astype(BF16)


def dot(a, b):
    return jnp.dot(a, b, preferred_element_type=F32)


def dot_rows(a, b):
    return lax.dot_general(a, b, (((1,), (1,)), ((), ())), preferred_element_type=F32)


def iota(shape, dim):
    return lax.broadcasted_iota(jnp.int32, shape, dim)


def small(index):
    return index.astype(F32).astype(BF16)


def merged_rows(a, b, part, swap=0):
    rows, width = a.shape
    first = small((iota((1, 16, width), 1) ^ swap * part) & (2 * part - 1)) < part
    a, b = a.reshape(rows // 16, 16, width), b.reshape(rows // 16, 16, width)
    return jnp.where(first, a, b).reshape(rows, width)


def turned(x):
    rows, width = x.shape
    return pltpu.roll(x.reshape(rows // 8, 8, width), 4, 1).reshape(rows, width)


def upper_half():
    return (lax.axis_index(AXES) >= lax.axis_size(AXES) // 2).astype(jnp.int32)


def pack_kernel(worker_hbm, label_hbm, emb_hbm, out_ref, place_ref, worker_ref, label_ref, emb, arrived):
    rows, width = emb.shape
    half = width // 2
    clusters = out_ref.shape[0] // 4
    pairs = clusters // 4
    fetches = [
        pltpu.make_async_copy(worker_hbm, worker_ref, arrived.at[0]),
        pltpu.make_async_copy(label_hbm, label_ref, arrived.at[1]),
        pltpu.make_async_copy(emb_hbm, emb, arrived.at[2]),
    ]
    for fetch in fetches:
        fetch.start()
    before = one_hot(iota((BLOCK, BLOCK), 0) < iota((BLOCK, BLOCK), 1))
    ones = jnp.ones((BLOCK, 128), BF16)
    line = small(iota((BLOCK, rows), 0))
    first_lane = iota((BLOCK, 128), 1) == 0
    fetches[0].wait()
    fetches[1].wait()
    worker = worker_ref[...].reshape(1, rows)
    label = label_ref[...].reshape(1, rows)
    side = label ^ upper_half()
    cluster = worker * SUB + side

    member = iota((clusters, rows), 0) == cluster
    member_hot = one_hot(member)
    count = jnp.zeros((clusters, 128), F32)
    earlier = []
    for part in range(0, rows, BLOCK):
        these = member_hot[:, part : part + BLOCK]
        inside = dot(these, before)
        earlier += [inside[:, k : k + 128] + count for k in range(0, BLOCK, 128)]
        count = count + dot(these, ones)
    earlier = jnp.concatenate(earlier, axis=1)
    rank = jnp.sum(jnp.where(member, earlier, 0.0), axis=0, keepdims=True).astype(jnp.int32)
    place_ref[...] = worker * 16 + label * PER_LABEL + rank
    total = count.astype(BF16)
    whole_row = jnp.where(rank < WHOLE, cluster * WHOLE + rank, -1)
    late_row = (worker & (pairs - 1)) * 8 + side * LATE + rank - WHOLE
    upper = (worker >= pairs).astype(jnp.int32)
    left_row = jnp.where(rank < WHOLE, -1, late_row + upper * 4)
    right_row = jnp.where(rank < WHOLE, -1, late_row + (1 - upper) * 4)
    fetches[2].wait()

    def chosen(block, target):
        inside = target - block * BLOCK
        inside = jnp.where((inside >= 0) & (inside < BLOCK), inside, -1)
        return jnp.where(line == small(inside), jnp.ones((), BF16), jnp.zeros((), BF16))

    def empty(spread, counts, slot):
        return jnp.where(first_lane & (dot(one_hot(spread), counts) <= slot.astype(F32)), MARK, 0.0)

    r, c = iota((BLOCK, 128), 0), iota((BLOCK, 128), 1)
    for block in range(pairs * 8 // BLOCK):
        left = dot(chosen(block, left_row), emb[:, :half])
        right = dot(chosen(block, right_row), emb[:, half:])
        left_sum = jnp.broadcast_to(jnp.sum(left * left, axis=1, keepdims=True), (BLOCK, 128))
        right_sum = jnp.broadcast_to(jnp.sum(right * right, axis=1, keepdims=True), (BLOCK, 128))
        left_scale = lax.rsqrt(left_sum + turned(right_sum) + 1e-06)[:, :1]
        right_scale = lax.rsqrt(right_sum + turned(left_sum) + 1e-06)[:, :1]
        per_block = BLOCK // 8 * SUB
        counts = [total[at + block * per_block :][:per_block] for at in (0, clusters // 2)]
        spread = c == (r >> 2 & 1) * per_block + (r >> 3) * SUB + (r >> 1 & 1)
        mark = empty(spread, jnp.concatenate(counts, axis=0), WHOLE + (r & 1))
        left = left * left_scale
        left = jnp.concatenate([left[:, :128] + mark, left[:, 128:]], axis=1).astype(BF16)
        right = (right * right_scale).astype(BF16)
        out_ref[pl.ds(block * BLOCK, BLOCK), width:] = merged_rows(left, right, 4)
        out_ref[pl.ds((block + pairs * 8 // BLOCK) * BLOCK, BLOCK), width:] = merged_rows(right, left, 4)
    r, c = iota((BLOCK, BLOCK // WHOLE), 0), iota((BLOCK, BLOCK // WHOLE), 1)
    for block in range(clusters * WHOLE // BLOCK):
        at = pl.ds(block * BLOCK, BLOCK)
        values = dot(chosen(block, whole_row), emb[...])
        values = values * lax.rsqrt(jnp.sum(values * values, axis=1, keepdims=True) + 1e-06)
        counts = total[block * BLOCK // WHOLE :][: BLOCK // WHOLE]
        mark = empty(c == r >> 2, counts, (iota((BLOCK, 128), 0) & 3))
        out_ref[at, :128] = (values[:, :128] + mark).astype(BF16)
        out_ref[at, 128:width] = values[:, 128:].astype(BF16)


def score_kernel(in_ref, out_ref, members):
    rows = in_ref.shape[0]
    devices = rows // 8
    count, width = members.shape[1:]
    half = width // 2
    wholes = devices * WHOLE

    for at in range(0, wholes, BLOCK):
        lower = in_ref[at : at + BLOCK, :width]
        upper = in_ref[wholes + at : wholes + at + BLOCK, :width]
        members[0, at : at + BLOCK, :] = merged_rows(lower, upper, 4)
        members[1, at : at + BLOCK, :] = merged_rows(upper, lower, 4)
    swap = upper_half()
    lates = wholes // 2
    quarters = [in_ref[k * lates : (k + 1) * lates, width:] for k in range(4)]
    for lab in range(SUB):
        near, far = [
            merged_rows(quarters[k + 2 * lab], quarters[k + 2 - 2 * lab], 2) for k in (0, 1)
        ]
        straight = merged_rows(near, far, 4)
        crossed = turned(merged_rows(far, near, 4).astype(F32)).astype(BF16)
        members[lab, wholes:, :half] = merged_rows(straight, crossed, 4, swap)
        members[lab, wholes:, half:] = merged_rows(crossed, straight, 4, swap)

    r, c = iota((BLOCK, BLOCK), 0), iota((BLOCK, BLOCK), 1)
    itself = jnp.where(r == c, -8.0, 0.0)
    sub, lane = iota((8, 128), 0), iota((8, 128), 1)
    source = (lane & 15) * 8 + sub

    def in_order(best, start, part, owner):
        total = jnp.zeros((8, 128), F32)
        for v in range(part // 16):
            these = jnp.broadcast_to(best[:, start + v * 128 : start + (v + 1) * 128], (8, 128))
            moved = jnp.take_along_axis(these, source, axis=1)
            total = total + jnp.where((lane >> 4) == owner * (part // 16) + v, moved, 0.0)
        return total

    blocks = count // BLOCK
    found = []
    for lab in range(SUB):
        parts = [members[lab, pl.ds(i * BLOCK, BLOCK), :] for i in range(blocks)]
        absent = [jnp.where(p[:, :128].astype(F32) > MARK - 0.5, -8.0, 0.0)[:, :1] for p in parts]
        absent_row = [jnp.broadcast_to(a, (BLOCK, 128)).T[:1] for a in absent]
        down, along = [[] for _ in parts], [[] for _ in parts]
        for i in range(blocks):
            for j in range(i, blocks):
                scores = dot_rows(parts[i], parts[j]) + absent[i]
                if i == j:
                    down[j].append(scores + itself)
                else:
                    down[j].append(scores)
                    scores = scores + absent_row[j]
                    along[i] += [scores[:, k : k + 128] for k in range(0, BLOCK, 128)]
        merged = []
        for i in range(blocks):
            best = jnp.max(functools.reduce(jnp.maximum, down[i]), axis=0, keepdims=True)
            if along[i]:
                other = functools.reduce(jnp.maximum, along[i]).T
                best = jnp.maximum(best, jnp.max(other, axis=0, keepdims=True))
            merged.append(jnp.where(best < -2.0, -1.0, best))
        best = jnp.concatenate(merged, axis=1)
        whole = in_order(best, 0, devices // 2, sub >> 2 ^ lab)
        whole = whole + pltpu.roll(whole, 4, 0)
        late = in_order(best, wholes, devices // 4, (sub >> 2) + ((sub >> 1 & 1) ^ lab) * 2)
        late = late + pltpu.roll(late, 4, 0)
        late = late + pltpu.roll(late, 2, 0)
        found += [whole[:WHOLE], late[:LATE]]
    found.append(jnp.zeros((128 - SUB * PER_LABEL, devices), F32))
    out_ref[...] = jnp.concatenate(found, axis=0).T


def unpack_kernel(place_ref, back_ref, out_ref):
    place = place_ref[...]
    rows = place.shape[1]
    back = back_ref[...]
    devices = back.shape[0]
    back = back.T[:16]
    high = back.astype(BF16)
    rest = back - high.astype(F32)
    middle = rest.astype(BF16)
    low = (rest - middle.astype(F32)).astype(BF16)
    chosen = one_hot(iota((devices, rows), 0) == place >> 4)
    values = dot(high, chosen) + dot(middle, chosen) + dot(low, chosen)
    mine = iota((16, rows), 0) == (place & 15)
    out_ref[...] = jnp.sum(jnp.where(mine, values, 0.0), axis=0)


VMEM = pl.BlockSpec(memory_space=pltpu.VMEM)
HBM = pl.BlockSpec(memory_space=pltpu.HBM)
PARAMS = pltpu.CompilerParams(vmem_limit_bytes=40 * 2**20)


def exchange(array):
    return lax.all_to_all(array, AXES, split_axis=0, concat_axis=0, tiled=True)


def local(embeddings, worker, label):
    rows, width = embeddings.shape
    devices = lax.axis_size("shard") * lax.axis_size("grp")
    shape = jax.ShapeDtypeStruct
    packed = (devices * 8, width * 3 // 2)
    in_hbm = [pltpu.with_memory_space_constraint(x, pltpu.HBM) for x in (worker, label, embeddings)]
    outgoing, place = pl.pallas_call(
        pack_kernel,
        out_shape=(shape(packed, BF16), shape((1, rows), jnp.int32)),
        in_specs=[HBM] * 3,
        out_specs=(VMEM, VMEM),
        scratch_shapes=[
            pltpu.VMEM((rows,), jnp.int32),
            pltpu.VMEM((rows,), jnp.int32),
            pltpu.VMEM((rows, width), BF16),
            pltpu.SemaphoreType.DMA((3,)),
        ],
        compiler_params=PARAMS,
        name="pack",
    )(*in_hbm)
    incoming = exchange(outgoing.reshape(devices, 8, packed[1])).reshape(packed)
    found = pl.pallas_call(
        score_kernel,
        out_shape=shape((devices, 128), F32),
        in_specs=[VMEM],
        out_specs=VMEM,
        scratch_shapes=[pltpu.VMEM((SUB, devices * PER_LABEL, width), BF16)],
        compiler_params=PARAMS,
        name="score",
    )(incoming)
    returned = exchange(found.reshape(devices, 1, 128)).reshape(devices, 128)
    return pl.pallas_call(
        unpack_kernel,
        out_shape=shape((rows,), F32),
        in_specs=[VMEM] * 2,
        out_specs=VMEM,
        compiler_params=PARAMS,
        name="unpack",
    )(place, returned)


def solution(mesh):
    return jax.shard_map(
        local,
        mesh=mesh,
        in_specs=(P(AXES, None), P(AXES), P(AXES)),
        out_specs=P(AXES),
        check_vma=False,
    )
```

```python
import functools

import jax
import jax.numpy as jnp
from jax import lax
from jax.experimental import pallas as pl
from jax.experimental.pallas import tpu as pltpu
from jax.sharding import PartitionSpec as P

SUB = 2
AXES = ("shard", "grp")
PER_LABEL = 6
WHOLE = 4
LATE = 2
BLOCK = 256
MARK = 2.0
BF16 = jnp.bfloat16
F32 = jnp.float32


def one_hot(flags):
    return jnp.where(flags, 1.0, 0.0).astype(BF16)


def dot(a, b):
    return jnp.dot(a, b, preferred_element_type=F32)


def dot_rows(a, b):
    return lax.dot_general(a, b, (((1,), (1,)), ((), ())), preferred_element_type=F32)


def iota(shape, dim):
    return lax.broadcasted_iota(jnp.int32, shape, dim)


def small(index):
    return index.astype(F32).astype(BF16)


def merged_rows(a, b, part, swap=0):
    rows, width = a.shape
    first = small((iota((1, 16, width), 1) ^ swap * part) & (2 * part - 1)) < part
    a, b = a.reshape(rows // 16, 16, width), b.reshape(rows // 16, 16, width)
    return jnp.where(first, a, b).reshape(rows, width)


def turned(x):
    rows, width = x.shape
    return pltpu.roll(x.reshape(rows // 8, 8, width), 4, 1).reshape(rows, width)


def upper_half():
    return (lax.axis_index(AXES) >= lax.axis_size(AXES) // 2).astype(jnp.int32)


def pack_kernel(worker_hbm, label_hbm, emb_hbm, out_ref, place_ref, worker_ref, label_ref, emb, arrived):
    rows, width = emb.shape
    half = width // 2
    clusters = out_ref.shape[0] // 4
    pairs = clusters // 4
    fetches = [
        pltpu.make_async_copy(worker_hbm, worker_ref, arrived.at[0]),
        pltpu.make_async_copy(label_hbm, label_ref, arrived.at[1]),
    ]
    bands = [(0, 256), (256, 512)]
    for i, (start, size) in enumerate(bands):
        at = pl.ds(start, size)
        fetches.append(pltpu.make_async_copy(emb_hbm.at[at], emb.at[at], arrived.at[2 + i]))
    for fetch in fetches[:3]:
        fetch.start()
    before = one_hot(iota((BLOCK, BLOCK), 0) < iota((BLOCK, BLOCK), 1))
    ones = jnp.ones((BLOCK, 128), BF16)
    line = small(iota((BLOCK, rows), 0))
    for fetch in fetches[3:]:
        fetch.start()
    fetches[0].wait()
    fetches[1].wait()
    worker = worker_ref[...].reshape(1, rows)
    label = label_ref[...].reshape(1, rows)
    side = label ^ upper_half()
    cluster = worker * SUB + side

    member = iota((clusters, rows), 0) == cluster
    member_hot = one_hot(member)
    count = jnp.zeros((clusters, 128), F32)
    earlier = []
    for part in range(0, rows, BLOCK):
        these = member_hot[:, part : part + BLOCK]
        inside = dot(these, before)
        earlier += [inside[:, k : k + 128] + count for k in range(0, BLOCK, 128)]
        count = count + dot(these, ones)
    earlier = jnp.concatenate(earlier, axis=1)
    rank = jnp.sum(jnp.where(member, earlier, 0.0), axis=0, keepdims=True).astype(jnp.int32)
    place_ref[...] = worker * 16 + label * PER_LABEL + rank
    total = count.astype(BF16)
    whole_row = jnp.where(rank < WHOLE, cluster * WHOLE + rank, -1)
    late_row = (worker & (pairs - 1)) * 8 + side * LATE + rank - WHOLE
    upper = (worker >= pairs).astype(jnp.int32)
    left_row = jnp.where(rank < WHOLE, -1, late_row + upper * 4)
    right_row = jnp.where(rank < WHOLE, -1, late_row + (1 - upper) * 4)
    def chosen(block, target):
        inside = target - block * BLOCK
        inside = jnp.where((inside >= 0) & (inside < BLOCK), inside, -1)
        return jnp.where(line == small(inside), jnp.ones((), BF16), jnp.zeros((), BF16))

    lane = iota((1, 128), 1)

    def filled(spread, counts):
        each = 128 // len(counts)
        merged = counts[0]
        for b in range(1, len(counts)):
            merged = jnp.where(small(lane) < small(jnp.full_like(lane, b * each)), merged, counts[b])
        return dot(one_hot(spread), merged)

    def empty(block, blocks, filled, slot):
        return jnp.where((lane == block * (128 // blocks)) & (filled <= slot.astype(F32)), MARK, 0.0)

    late_blocks = range(pairs * 8 // BLOCK)
    jobs = [(block, target, k * half, half) for block in late_blocks for k, target in enumerate((left_row, right_row))]
    hot = [chosen(block, target) for block, target, _, _ in jobs]
    sums = [0.0] * len(jobs)
    for i, (start, size) in enumerate(bands):
        fetches[2 + i].wait()
        for n, (_, _, column, columns) in enumerate(jobs):
            part = dot(hot[n][:, start : start + size], emb[start : start + size, column : column + columns])
            sums[n] = part if i == 0 else sums[n] + part

    r, c = iota((BLOCK, 128), 0), iota((BLOCK, 128), 1)
    blocks = pairs * 8 // BLOCK
    per_block = BLOCK // 8 * SUB
    spread = c == (r >> 2 & 1) * per_block + (r >> 3) * SUB + (r >> 1 & 1)
    counts = [
        [total[at + block * per_block :][:per_block] for at in (0, clusters // 2)]
        for block in range(blocks)
    ]
    late_filled = filled(spread, [jnp.concatenate(x, axis=0) for x in counts])
    late_slot = WHOLE + (r & 1)
    for block in range(blocks):
        left, right = sums[2 * block], sums[2 * block + 1]
        left_sum = jnp.broadcast_to(jnp.sum(left * left, axis=1, keepdims=True), (BLOCK, 128))
        right_sum = jnp.broadcast_to(jnp.sum(right * right, axis=1, keepdims=True), (BLOCK, 128))
        left_scale = lax.rsqrt(left_sum + turned(right_sum) + 1e-06)[:, :1]
        right_scale = lax.rsqrt(right_sum + turned(left_sum) + 1e-06)[:, :1]
        mark = empty(block, blocks, late_filled, late_slot)
        left = left * left_scale
        left = jnp.concatenate([left[:, :128] + mark, left[:, 128:]], axis=1).astype(BF16)
        right = (right * right_scale).astype(BF16)
        out_ref[pl.ds(block * BLOCK, BLOCK), width:] = merged_rows(left, right, 4)
        out_ref[pl.ds((block + pairs * 8 // BLOCK) * BLOCK, BLOCK), width:] = merged_rows(right, left, 4)
    r, c = iota((BLOCK, BLOCK // WHOLE), 0), iota((BLOCK, BLOCK // WHOLE), 1)
    blocks = clusters * WHOLE // BLOCK
    counts = [total[block * BLOCK // WHOLE :][: BLOCK // WHOLE] for block in range(blocks)]
    whole_filled = filled(c == r >> 2, counts)
    whole_slot = iota((BLOCK, 128), 0) & 3
    for block in range(blocks):
        at = pl.ds(block * BLOCK, BLOCK)
        values = dot(chosen(block, whole_row), emb[...])
        values = values * lax.rsqrt(jnp.sum(values * values, axis=1, keepdims=True) + 1e-06)
        mark = empty(block, blocks, whole_filled, whole_slot)
        out_ref[at, :128] = (values[:, :128] + mark).astype(BF16)
        out_ref[at, 128:width] = values[:, 128:].astype(BF16)


def score_kernel(in_ref, out_ref, members):
    rows = in_ref.shape[0]
    devices = rows // 8
    count, width = members.shape[1:]
    half = width // 2
    wholes = devices * WHOLE

    swap = upper_half()
    lates = wholes // 2
    quarters = [in_ref[k * lates : (k + 1) * lates, width:] for k in range(4)]
    r, c = iota((BLOCK, BLOCK), 0), iota((BLOCK, BLOCK), 1)
    itself = jnp.where(r == c, -8.0, 0.0)
    sub, lane = iota((8, 128), 0), iota((8, 128), 1)
    source = (lane & 15) * 8 + sub

    def in_order(best, start, part, owner):
        total = jnp.zeros((8, 128), F32)
        for v in range(part // 16):
            these = jnp.broadcast_to(best[:, start + v * 128 : start + (v + 1) * 128], (8, 128))
            moved = jnp.take_along_axis(these, source, axis=1)
            total = total + jnp.where((lane >> 4) == owner * (part // 16) + v, moved, 0.0)
        return total

    blocks = count // BLOCK
    found = []
    for lab in range(SUB):
        for at in range(0, wholes, BLOCK):
            halves = [in_ref[k * wholes + at : k * wholes + at + BLOCK, :width] for k in (lab, 1 - lab)]
            members[lab, at : at + BLOCK, :] = merged_rows(*halves, 4)
        near, far = [
            merged_rows(quarters[k + 2 * lab], quarters[k + 2 - 2 * lab], 2) for k in (0, 1)
        ]
        straight = merged_rows(near, far, 4)
        crossed = turned(merged_rows(far, near, 4).astype(F32)).astype(BF16)
        members[lab, wholes:, :half] = merged_rows(straight, crossed, 4, swap)
        members[lab, wholes:, half:] = merged_rows(crossed, straight, 4, swap)
        parts = [members[lab, pl.ds(i * BLOCK, BLOCK), :] for i in range(blocks)]
        absent = [
            jnp.min(jnp.where(p[:, :128].astype(F32) > MARK - 0.5, -8.0, 0.0), axis=1, keepdims=True)
            for p in parts
        ]
        absent_row = [jnp.broadcast_to(a, (BLOCK, 128)).T[:1] for a in absent]
        down, along = [[] for _ in parts], [[] for _ in parts]
        for i in range(blocks):
            for j in range(i, blocks):
                scores = dot_rows(parts[i], parts[j]) + absent[i]
                if i == j:
                    down[j].append(scores + itself)
                else:
                    down[j].append(scores)
                    scores = scores + absent_row[j]
                    along[i] += [scores[:, k : k + 128] for k in range(0, BLOCK, 128)]
        merged = []
        for i in range(blocks):
            best = jnp.max(functools.reduce(jnp.maximum, down[i]), axis=0, keepdims=True)
            if along[i]:
                other = functools.reduce(jnp.maximum, along[i]).T
                best = jnp.maximum(best, jnp.max(other, axis=0, keepdims=True))
            merged.append(jnp.where(best < -2.0, -1.0, best))
        best = jnp.concatenate(merged, axis=1)
        whole = in_order(best, 0, devices // 2, sub >> 2 ^ lab)
        whole = whole + pltpu.roll(whole, 4, 0)
        late = in_order(best, wholes, devices // 4, (sub >> 2) + ((sub >> 1 & 1) ^ lab) * 2)
        late = late + pltpu.roll(late, 4, 0)
        late = late + pltpu.roll(late, 2, 0)
        found += [whole[:WHOLE], late[:LATE]]
    found.append(jnp.zeros((128 - SUB * PER_LABEL, devices), F32))
    out_ref[...] = jnp.concatenate(found, axis=0).T


def unpack_kernel(place_ref, back_ref, out_ref):
    place = place_ref[...]
    rows = place.shape[1]
    back = back_ref[...]
    devices = back.shape[0]
    back = back.T[:16]
    high = back.astype(BF16)
    rest = back - high.astype(F32)
    middle = rest.astype(BF16)
    low = (rest - middle.astype(F32)).astype(BF16)
    chosen = one_hot(iota((devices, rows), 0) == place >> 4)
    values = dot(high, chosen) + dot(middle, chosen) + dot(low, chosen)
    mine = iota((16, rows), 0) == (place & 15)
    out_ref[...] = jnp.sum(jnp.where(mine, values, 0.0), axis=0)


VMEM = pl.BlockSpec(memory_space=pltpu.VMEM)
HBM = pl.BlockSpec(memory_space=pltpu.HBM)
PARAMS = pltpu.CompilerParams(vmem_limit_bytes=40 * 2**20)


def exchange(array):
    return lax.all_to_all(array, AXES, split_axis=0, concat_axis=0, tiled=True)


def local(embeddings, worker, label):
    rows, width = embeddings.shape
    devices = lax.axis_size("shard") * lax.axis_size("grp")
    shape = jax.ShapeDtypeStruct
    packed = (devices * 8, width * 3 // 2)
    in_hbm = [pltpu.with_memory_space_constraint(x, pltpu.HBM) for x in (worker, label, embeddings)]
    outgoing, place = pl.pallas_call(
        pack_kernel,
        out_shape=(shape(packed, BF16), shape((1, rows), jnp.int32)),
        in_specs=[HBM] * 3,
        out_specs=(VMEM, VMEM),
        scratch_shapes=[
            pltpu.VMEM((rows,), jnp.int32),
            pltpu.VMEM((rows,), jnp.int32),
            pltpu.VMEM((rows, width), BF16),
            pltpu.SemaphoreType.DMA((4,)),
        ],
        compiler_params=PARAMS,
        name="pack",
    )(*in_hbm)
    incoming = exchange(outgoing.reshape(devices, 8, packed[1])).reshape(packed)
    found = pl.pallas_call(
        score_kernel,
        out_shape=shape((devices, 128), F32),
        in_specs=[VMEM],
        out_specs=VMEM,
        scratch_shapes=[pltpu.VMEM((SUB, devices * PER_LABEL, width), BF16)],
        compiler_params=PARAMS,
        name="score",
    )(incoming)
    returned = exchange(found.reshape(devices, 1, 128)).reshape(devices, 128)
    return pl.pallas_call(
        unpack_kernel,
        out_shape=shape((rows,), F32),
        in_specs=[VMEM] * 2,
        out_specs=VMEM,
        compiler_params=PARAMS,
        name="unpack",
    )(place, returned)


def solution(mesh):
    return jax.shard_map(
        local,
        mesh=mesh,
        in_specs=(P(AXES, None), P(AXES), P(AXES)),
        out_specs=P(AXES),
        check_vma=False,
    )
```

```python
import functools

import jax
import jax.numpy as jnp
from jax import lax
from jax.experimental import pallas as pl
from jax.experimental.pallas import tpu as pltpu
from jax.sharding import PartitionSpec as P

SUB = 2
AXES = ("shard", "grp")
PER_LABEL = 6
WHOLE = 4
LATE = 2
BLOCK = 256
MARK = 2.0
BF16 = jnp.bfloat16
F32 = jnp.float32


def one_hot(flags):
    return jnp.where(flags, 1.0, 0.0).astype(BF16)


def dot(a, b):
    return jnp.dot(a, b, preferred_element_type=F32)


def dot_rows(a, b):
    return lax.dot_general(a, b, (((1,), (1,)), ((), ())), preferred_element_type=F32)


def iota(shape, dim):
    return lax.broadcasted_iota(jnp.int32, shape, dim)


def small(index):
    return index.astype(F32).astype(BF16)


def merged_rows(a, b, part, swap=0):
    rows, width = a.shape
    first = small((iota((1, 16, width), 1) ^ swap * part) & (2 * part - 1)) < part
    a, b = a.reshape(rows // 16, 16, width), b.reshape(rows // 16, 16, width)
    return jnp.where(first, a, b).reshape(rows, width)


def turned(x):
    rows, width = x.shape
    return pltpu.roll(x.reshape(rows // 8, 8, width), 4, 1).reshape(rows, width)


def upper_half():
    return (lax.axis_index(AXES) >= lax.axis_size(AXES) // 2).astype(jnp.int32)


def pack_kernel(worker_hbm, label_hbm, emb_hbm, out_ref, place_ref, worker_ref, label_ref, emb, arrived):
    rows, width = emb.shape
    half = width // 2
    clusters = out_ref.shape[0] // 4
    pairs = clusters // 4
    fetches = [
        pltpu.make_async_copy(worker_hbm, worker_ref, arrived.at[0]),
        pltpu.make_async_copy(label_hbm, label_ref, arrived.at[1]),
    ]
    bands = [(0, 256), (256, 256), (512, 256)]
    for i, (start, size) in enumerate(bands):
        at = pl.ds(start, size)
        fetches.append(pltpu.make_async_copy(emb_hbm.at[at], emb.at[at], arrived.at[2 + i]))
    for fetch in fetches[:3]:
        fetch.start()
    before = one_hot(iota((BLOCK, BLOCK), 0) < iota((BLOCK, BLOCK), 1))
    ones = jnp.ones((BLOCK, 128), BF16)
    line = small(iota((BLOCK, rows), 0))
    for fetch in fetches[3:]:
        fetch.start()
    fetches[0].wait()
    fetches[1].wait()
    worker = worker_ref[...].reshape(1, rows)
    label = label_ref[...].reshape(1, rows)
    side = label ^ upper_half()
    cluster = worker * SUB + side

    member = iota((clusters, rows), 0) == cluster
    member_hot = one_hot(member)
    count = jnp.zeros((clusters, 128), F32)
    earlier = []
    for part in range(0, rows, BLOCK):
        these = member_hot[:, part : part + BLOCK]
        inside = dot(these, before)
        earlier += [inside[:, k : k + 128] + count for k in range(0, BLOCK, 128)]
        count = count + dot(these, ones)
    earlier = jnp.concatenate(earlier, axis=1)
    rank = jnp.sum(jnp.where(member, earlier, 0.0), axis=0, keepdims=True).astype(jnp.int32)
    place_ref[...] = worker * 16 + label * PER_LABEL + rank
    total = count.astype(BF16)
    whole_row = jnp.where(rank < WHOLE, cluster * WHOLE + rank, -1)
    late_row = (worker & (pairs - 1)) * 8 + side * LATE + rank - WHOLE
    upper = (worker >= pairs).astype(jnp.int32)
    left_row = jnp.where(rank < WHOLE, -1, late_row + upper * 4)
    right_row = jnp.where(rank < WHOLE, -1, late_row + (1 - upper) * 4)
    def chosen(block, target):
        inside = target - block * BLOCK
        inside = jnp.where((inside >= 0) & (inside < BLOCK), inside, -1)
        return jnp.where(line == small(inside), jnp.ones((), BF16), jnp.zeros((), BF16))

    lane = iota((1, 128), 1)

    def filled(spread, counts):
        each = 128 // len(counts)
        merged = counts[0]
        for b in range(1, len(counts)):
            merged = jnp.where(small(lane) < small(jnp.full_like(lane, b * each)), merged, counts[b])
        return dot(one_hot(spread), merged)

    def empty(block, blocks, filled, slot):
        return jnp.where((lane == block * (128 // blocks)) & (filled <= slot.astype(F32)), MARK, 0.0)

    late_blocks = range(pairs * 8 // BLOCK)
    jobs = [(block, target, k * half, half) for block in late_blocks for k, target in enumerate((left_row, right_row))]
    hot = [chosen(block, target) for block, target, _, _ in jobs]
    sums = [0.0] * len(jobs)
    for i, (start, size) in enumerate(bands):
        fetches[2 + i].wait()
        for n, (_, _, column, columns) in enumerate(jobs):
            part = dot(hot[n][:, start : start + size], emb[start : start + size, column : column + columns])
            sums[n] = part if i == 0 else sums[n] + part

    r, c = iota((BLOCK, 128), 0), iota((BLOCK, 128), 1)
    blocks = pairs * 8 // BLOCK
    per_block = BLOCK // 8 * SUB
    spread = c == (r >> 2 & 1) * per_block + (r >> 3) * SUB + (r >> 1 & 1)
    counts = [
        [total[at + block * per_block :][:per_block] for at in (0, clusters // 2)]
        for block in range(blocks)
    ]
    late_filled = filled(spread, [jnp.concatenate(x, axis=0) for x in counts])
    late_slot = WHOLE + (r & 1)
    for block in range(blocks):
        left, right = sums[2 * block], sums[2 * block + 1]
        left_sum = jnp.broadcast_to(jnp.sum(left * left, axis=1, keepdims=True), (BLOCK, 128))
        right_sum = jnp.broadcast_to(jnp.sum(right * right, axis=1, keepdims=True), (BLOCK, 128))
        left_scale = lax.rsqrt(left_sum + turned(right_sum) + 1e-06)[:, :1]
        right_scale = lax.rsqrt(right_sum + turned(left_sum) + 1e-06)[:, :1]
        mark = empty(block, blocks, late_filled, late_slot)
        left = left * left_scale
        left = jnp.concatenate([left[:, :128] + mark, left[:, 128:]], axis=1).astype(BF16)
        right = (right * right_scale).astype(BF16)
        out_ref[pl.ds(block * BLOCK, BLOCK), width:] = merged_rows(left, right, 4)
        out_ref[pl.ds((block + pairs * 8 // BLOCK) * BLOCK, BLOCK), width:] = merged_rows(right, left, 4)
    r, c = iota((BLOCK, BLOCK // WHOLE), 0), iota((BLOCK, BLOCK // WHOLE), 1)
    blocks = clusters * WHOLE // BLOCK
    counts = [total[block * BLOCK // WHOLE :][: BLOCK // WHOLE] for block in range(blocks)]
    whole_filled = filled(c == r >> 2, counts)
    whole_slot = iota((BLOCK, 128), 0) & 3
    for block in range(blocks):
        at = pl.ds(block * BLOCK, BLOCK)
        values = dot(chosen(block, whole_row), emb[...])
        values = values * lax.rsqrt(jnp.sum(values * values, axis=1, keepdims=True) + 1e-06)
        mark = empty(block, blocks, whole_filled, whole_slot)
        out_ref[at, :128] = (values[:, :128] + mark).astype(BF16)
        out_ref[at, 128:width] = values[:, 128:].astype(BF16)


def score_kernel(in_ref, out_ref, members):
    rows = in_ref.shape[0]
    devices = rows // 8
    count, width = members.shape[1:]
    half = width // 2
    wholes = devices * WHOLE

    swap = upper_half()
    lates = wholes // 2
    quarters = [in_ref[k * lates : (k + 1) * lates, width:] for k in range(4)]
    r, c = iota((BLOCK, BLOCK), 0), iota((BLOCK, BLOCK), 1)
    itself = jnp.where(r == c, -8.0, 0.0)
    sub, lane = iota((8, 128), 0), iota((8, 128), 1)
    source = (lane & 15) * 8 + sub

    def in_order(best, start, part, owner):
        total = jnp.zeros((8, 128), F32)
        for v in range(part // 16):
            these = jnp.broadcast_to(best[:, start + v * 128 : start + (v + 1) * 128], (8, 128))
            moved = jnp.take_along_axis(these, source, axis=1)
            total = total + jnp.where((lane >> 4) == owner * (part // 16) + v, moved, 0.0)
        return total

    blocks = count // BLOCK
    found = []
    for lab in range(SUB):
        for at in range(0, wholes, BLOCK):
            halves = [in_ref[k * wholes + at : k * wholes + at + BLOCK, :width] for k in (lab, 1 - lab)]
            members[lab, at : at + BLOCK, :] = merged_rows(*halves, 4)
        near, far = [
            merged_rows(quarters[k + 2 * lab], quarters[k + 2 - 2 * lab], 2) for k in (0, 1)
        ]
        straight = merged_rows(near, far, 4)
        crossed = turned(merged_rows(far, near, 4).astype(F32)).astype(BF16)
        members[lab, wholes:, :half] = merged_rows(straight, crossed, 4, swap)
        members[lab, wholes:, half:] = merged_rows(crossed, straight, 4, swap)
        parts = [members[lab, pl.ds(i * BLOCK, BLOCK), :] for i in range(blocks)]
        absent = [
            jnp.min(jnp.where(p[:, :128].astype(F32) > MARK - 0.5, -8.0, 0.0), axis=1, keepdims=True)
            for p in parts
        ]
        absent_row = [jnp.broadcast_to(a, (BLOCK, 128)).T[:1] for a in absent]
        down, along = [[] for _ in parts], [[] for _ in parts]
        for i in range(blocks):
            for j in range(i, blocks):
                scores = dot_rows(parts[i], parts[j]) + absent[i]
                if i == j:
                    down[j].append(scores + itself)
                else:
                    down[j].append(scores)
                    scores = scores + absent_row[j]
                    along[i] += [scores[:, k : k + 128] for k in range(0, BLOCK, 128)]
        merged = []
        for i in range(blocks):
            best = jnp.max(functools.reduce(jnp.maximum, down[i]), axis=0, keepdims=True)
            if along[i]:
                other = functools.reduce(jnp.maximum, along[i]).T
                best = jnp.maximum(best, jnp.max(other, axis=0, keepdims=True))
            merged.append(jnp.where(best < -2.0, -1.0, best))
        best = jnp.concatenate(merged, axis=1)
        whole = in_order(best, 0, devices // 2, sub >> 2 ^ lab)
        whole = whole + pltpu.roll(whole, 4, 0)
        late = in_order(best, wholes, devices // 4, (sub >> 2) + ((sub >> 1 & 1) ^ lab) * 2)
        late = late + pltpu.roll(late, 4, 0)
        late = late + pltpu.roll(late, 2, 0)
        found += [whole[:WHOLE], late[:LATE]]
    found.append(jnp.zeros((128 - SUB * PER_LABEL, devices), F32))
    out_ref[...] = jnp.concatenate(found, axis=0).T


def unpack_kernel(place_ref, back_ref, out_ref):
    place = place_ref[...]
    rows = place.shape[1]
    back = back_ref[...]
    devices = back.shape[0]
    back = back.T[:16]
    high = back.astype(BF16)
    rest = back - high.astype(F32)
    middle = rest.astype(BF16)
    low = (rest - middle.astype(F32)).astype(BF16)
    chosen = one_hot(iota((devices, rows), 0) == place >> 4)
    values = dot(jnp.concatenate([high, middle, low], axis=0), chosen)
    values = values[:16] + values[16:32] + values[32:]
    mine = iota((16, rows), 0) == (place & 15)
    out_ref[...] = jnp.sum(jnp.where(mine, values, 0.0), axis=0)


VMEM = pl.BlockSpec(memory_space=pltpu.VMEM)
HBM = pl.BlockSpec(memory_space=pltpu.HBM)
PARAMS = pltpu.CompilerParams(vmem_limit_bytes=40 * 2**20)


def exchange(array):
    return lax.all_to_all(array, AXES, split_axis=0, concat_axis=0, tiled=True)


def local(embeddings, worker, label):
    rows, width = embeddings.shape
    devices = lax.axis_size("shard") * lax.axis_size("grp")
    shape = jax.ShapeDtypeStruct
    packed = (devices * 8, width * 3 // 2)
    in_hbm = [pltpu.with_memory_space_constraint(x, pltpu.HBM) for x in (worker, label, embeddings)]
    outgoing, place = pl.pallas_call(
        pack_kernel,
        out_shape=(shape(packed, BF16), shape((1, rows), jnp.int32)),
        in_specs=[HBM] * 3,
        out_specs=(VMEM, VMEM),
        scratch_shapes=[
            pltpu.VMEM((rows,), jnp.int32),
            pltpu.VMEM((rows,), jnp.int32),
            pltpu.VMEM((rows, width), BF16),
            pltpu.SemaphoreType.DMA((5,)),
        ],
        compiler_params=PARAMS,
        name="pack",
    )(*in_hbm)
    incoming = exchange(outgoing.reshape(devices, 8, packed[1])).reshape(packed)
    found = pl.pallas_call(
        score_kernel,
        out_shape=shape((devices, 128), F32),
        in_specs=[VMEM],
        out_specs=VMEM,
        scratch_shapes=[pltpu.VMEM((SUB, devices * PER_LABEL, width), BF16)],
        compiler_params=PARAMS,
        name="score",
    )(incoming)
    returned = exchange(found.reshape(devices, 1, 128)).reshape(devices, 128)
    return pl.pallas_call(
        unpack_kernel,
        out_shape=shape((rows,), F32),
        in_specs=[VMEM] * 2,
        out_specs=VMEM,
        compiler_params=PARAMS,
        name="unpack",
    )(place, returned)


def solution(mesh):
    return jax.shard_map(
        local,
        mesh=mesh,
        in_specs=(P(AXES, None), P(AXES), P(AXES)),
        out_specs=P(AXES),
        check_vma=False,
    )
```

```python
import functools

import jax
import jax.numpy as jnp
from jax import lax
from jax.experimental import pallas as pl
from jax.experimental.pallas import tpu as pltpu
from jax.sharding import PartitionSpec as P

SUB = 2
AXES = ("shard", "grp")
PER_LABEL = 6
WHOLE = 4
LATE = 2
BLOCK = 256
MARK = 2.0
BF16 = jnp.bfloat16
F32 = jnp.float32


def one_hot(flags):
    return jnp.where(flags, 1.0, 0.0).astype(BF16)


def dot(a, b):
    return jnp.dot(a, b, preferred_element_type=F32)


def dot_rows(a, b):
    return lax.dot_general(a, b, (((1,), (1,)), ((), ())), preferred_element_type=F32)


def iota(shape, dim):
    return lax.broadcasted_iota(jnp.int32, shape, dim)


def small(index):
    return index.astype(F32).astype(BF16)


def merged_rows(a, b, part, swap=0):
    rows, width = a.shape
    first = small((iota((1, 16, width), 1) ^ swap * part) & (2 * part - 1)) < part
    a, b = a.reshape(rows // 16, 16, width), b.reshape(rows // 16, 16, width)
    return jnp.where(first, a, b).reshape(rows, width)


def turned(x):
    rows, width = x.shape
    return pltpu.roll(x.reshape(rows // 8, 8, width), 4, 1).reshape(rows, width)


def upper_half():
    return (lax.axis_index(AXES) >= lax.axis_size(AXES) // 2).astype(jnp.int32)


def pack_kernel(worker_hbm, label_hbm, emb_hbm, out_ref, place_ref, worker_ref, label_ref, emb, arrived):
    rows, width = emb.shape
    half = width // 2
    clusters = out_ref.shape[0] // 4
    pairs = clusters // 4
    fetches = [
        pltpu.make_async_copy(worker_hbm, worker_ref, arrived.at[0]),
        pltpu.make_async_copy(label_hbm, label_ref, arrived.at[1]),
    ]
    bands = [(0, 256), (256, 256), (512, 256)]
    for i, (start, size) in enumerate(bands):
        at = pl.ds(start, size)
        fetches.append(pltpu.make_async_copy(emb_hbm.at[at], emb.at[at], arrived.at[2 + i]))
    for fetch in fetches[:3]:
        fetch.start()
    before = one_hot(iota((BLOCK, BLOCK), 0) < iota((BLOCK, BLOCK), 1))
    ones = jnp.ones((BLOCK, 128), BF16)
    line = small(iota((BLOCK, rows), 0))
    for fetch in fetches[3:]:
        fetch.start()
    fetches[0].wait()
    fetches[1].wait()
    worker = worker_ref[...].reshape(1, rows)
    label = label_ref[...].reshape(1, rows)
    side = label ^ upper_half()
    cluster = worker * SUB + side

    member = iota((clusters, rows), 0) == cluster
    member_hot = one_hot(member)
    count = jnp.zeros((clusters, 128), F32)
    earlier = []
    for part in range(0, rows, BLOCK):
        these = member_hot[:, part : part + BLOCK]
        inside = dot(these, before)
        earlier += [inside[:, k : k + 128] + count for k in range(0, BLOCK, 128)]
        count = count + dot(these, ones)
    earlier = jnp.concatenate(earlier, axis=1)
    rank = jnp.sum(jnp.where(member, earlier, 0.0), axis=0, keepdims=True).astype(jnp.int32)
    place_ref[...] = worker * 16 + label * PER_LABEL + rank
    total = count.astype(BF16)
    whole_row = jnp.where(rank < WHOLE, cluster * WHOLE + rank, -1)
    late_row = (worker & (pairs - 1)) * 8 + side * LATE + rank - WHOLE
    upper = (worker >= pairs).astype(jnp.int32)
    left_row = jnp.where(rank < WHOLE, -1, late_row + upper * 4)
    right_row = jnp.where(rank < WHOLE, -1, late_row + (1 - upper) * 4)
    def chosen(block, target):
        inside = target - block * BLOCK
        inside = jnp.where((inside >= 0) & (inside < BLOCK), inside, -1)
        return jnp.where(line == small(inside), jnp.ones((), BF16), jnp.zeros((), BF16))

    lane = iota((1, 128), 1)

    def filled(spread, counts):
        each = 128 // len(counts)
        merged = counts[0]
        for b in range(1, len(counts)):
            merged = jnp.where(small(lane) < small(jnp.full_like(lane, b * each)), merged, counts[b])
        return dot(one_hot(spread), merged)

    def empty(block, blocks, filled, slot):
        return jnp.where((lane == block * (128 // blocks)) & (filled <= slot.astype(F32)), MARK, 0.0)

    late_blocks = range(pairs * 8 // BLOCK)
    jobs = [(block, target, k * half, half) for block in late_blocks for k, target in enumerate((left_row, right_row))]
    hot = [chosen(block, target) for block, target, _, _ in jobs]
    sums = [0.0] * len(jobs)
    for i, (start, size) in enumerate(bands):
        fetches[2 + i].wait()
        for n, (_, _, column, columns) in enumerate(jobs):
            part = dot(hot[n][:, start : start + size], emb[start : start + size, column : column + columns])
            sums[n] = part if i == 0 else sums[n] + part

    r, c = iota((BLOCK, 128), 0), iota((BLOCK, 128), 1)
    blocks = pairs * 8 // BLOCK
    per_block = BLOCK // 8 * SUB
    spread = c == (r >> 2 & 1) * per_block + (r >> 3) * SUB + (r >> 1 & 1)
    counts = [
        [total[at + block * per_block :][:per_block] for at in (0, clusters // 2)]
        for block in range(blocks)
    ]
    late_filled = filled(spread, [jnp.concatenate(x, axis=0) for x in counts])
    late_slot = WHOLE + (r & 1)
    for block in range(blocks):
        left, right = sums[2 * block], sums[2 * block + 1]
        left_sum = jnp.broadcast_to(jnp.sum(left * left, axis=1, keepdims=True), (BLOCK, 128))
        right_sum = jnp.broadcast_to(jnp.sum(right * right, axis=1, keepdims=True), (BLOCK, 128))
        left_scale = lax.rsqrt(left_sum + turned(right_sum) + 1e-06)[:, :1]
        right_scale = lax.rsqrt(right_sum + turned(left_sum) + 1e-06)[:, :1]
        mark = empty(block, blocks, late_filled, late_slot)
        left = left * left_scale
        left = jnp.concatenate([left[:, :128] + mark, left[:, 128:]], axis=1).astype(BF16)
        right = (right * right_scale).astype(BF16)
        out_ref[pl.ds(block * BLOCK, BLOCK), width:] = merged_rows(left, right, 4)
        out_ref[pl.ds((block + pairs * 8 // BLOCK) * BLOCK, BLOCK), width:] = merged_rows(right, left, 4)
    r, c = iota((BLOCK, BLOCK // WHOLE), 0), iota((BLOCK, BLOCK // WHOLE), 1)
    blocks = clusters * WHOLE // BLOCK
    counts = [total[block * BLOCK // WHOLE :][: BLOCK // WHOLE] for block in range(blocks)]
    whole_filled = filled(c == r >> 2, counts)
    whole_slot = iota((BLOCK, 128), 0) & 3
    for block in range(blocks):
        at = pl.ds(block * BLOCK, BLOCK)
        values = dot(chosen(block, whole_row), emb[...])
        values = values * lax.rsqrt(jnp.sum(values * values, axis=1, keepdims=True) + 1e-06)
        mark = empty(block, blocks, whole_filled, whole_slot)
        out_ref[at, :128] = (values[:, :128] + mark).astype(BF16)
        out_ref[at, 128:width] = values[:, 128:].astype(BF16)


def score_kernel(in_ref, out_ref, members):
    rows = in_ref.shape[0]
    devices = rows // 8
    count, width = members.shape[1:]
    half = width // 2
    wholes = devices * WHOLE

    swap = upper_half()
    lates = wholes // 2
    quarters = [in_ref[k * lates : (k + 1) * lates, width:] for k in range(4)]
    r, c = iota((BLOCK, BLOCK), 0), iota((BLOCK, BLOCK), 1)
    itself = jnp.where(r == c, -8.0, 0.0)
    sub, lane = iota((8, 128), 0), iota((8, 128), 1)
    source = (lane & 15) * 8 + sub

    def in_order(best, start, part, owner):
        total = jnp.zeros((8, 128), F32)
        for v in range(part // 16):
            these = jnp.broadcast_to(best[:, start + v * 128 : start + (v + 1) * 128], (8, 128))
            moved = jnp.take_along_axis(these, source, axis=1)
            total = total + jnp.where((lane >> 4) == owner * (part // 16) + v, moved, 0.0)
        return total

    blocks = count // BLOCK
    found = []
    for lab in range(SUB):
        for at in range(0, wholes, BLOCK):
            halves = [in_ref[k * wholes + at : k * wholes + at + BLOCK, :width] for k in (lab, 1 - lab)]
            members[lab, at : at + BLOCK, :] = merged_rows(*halves, 4)
        near, far = [
            merged_rows(quarters[k + 2 * lab], quarters[k + 2 - 2 * lab], 2) for k in (0, 1)
        ]
        straight = merged_rows(near, far, 4)
        crossed = turned(merged_rows(far, near, 4).astype(F32)).astype(BF16)
        members[lab, wholes:, :half] = merged_rows(straight, crossed, 4, swap)
        members[lab, wholes:, half:] = merged_rows(crossed, straight, 4, swap)
        parts = [members[lab, pl.ds(i * BLOCK, BLOCK), :] for i in range(blocks)]
        absent = [
            jnp.min(jnp.where(p[:, :128].astype(F32) > MARK - 0.5, -8.0, 0.0), axis=1, keepdims=True)
            for p in parts
        ]
        absent_row = [jnp.broadcast_to(a, (BLOCK, 128)).T[:1] for a in absent]
        down, along = [[] for _ in parts], [[] for _ in parts]
        for j in reversed(range(blocks)):
            stacked = dot_rows(members[lab, : (j + 1) * BLOCK, :], parts[j])
            for i in range(j + 1):
                scores = stacked[i * BLOCK : (i + 1) * BLOCK] + absent[i]
                if i == j:
                    down[j].append(scores + itself)
                else:
                    down[j].append(scores)
                    scores = scores + absent_row[j]
                    along[i] += [scores[:, k : k + 128] for k in range(0, BLOCK, 128)]
        merged = []
        for i in range(blocks):
            best = jnp.max(functools.reduce(jnp.maximum, down[i]), axis=0, keepdims=True)
            if along[i]:
                other = functools.reduce(jnp.maximum, along[i]).T
                best = jnp.maximum(best, jnp.max(other, axis=0, keepdims=True))
            merged.append(jnp.where(best < -2.0, -1.0, best))
        best = jnp.concatenate(merged, axis=1)
        whole = in_order(best, 0, devices // 2, sub >> 2 ^ lab)
        whole = whole + pltpu.roll(whole, 4, 0)
        late = in_order(best, wholes, devices // 4, (sub >> 2) + ((sub >> 1 & 1) ^ lab) * 2)
        late = late + pltpu.roll(late, 4, 0)
        late = late + pltpu.roll(late, 2, 0)
        found += [whole[:WHOLE], late[:LATE]]
    found.append(jnp.zeros((128 - SUB * PER_LABEL, devices), F32))
    out_ref[...] = jnp.concatenate(found, axis=0).T


def unpack_kernel(place_ref, back_ref, out_ref):
    place = place_ref[...]
    rows = place.shape[1]
    back = back_ref[...]
    devices = back.shape[0]
    back = back.T[:16]
    high = back.astype(BF16)
    rest = back - high.astype(F32)
    middle = rest.astype(BF16)
    low = (rest - middle.astype(F32)).astype(BF16)
    chosen = one_hot(iota((devices, rows), 0) == place >> 4)
    values = dot(jnp.concatenate([high, middle, low], axis=0), chosen)
    values = values[:16] + values[16:32] + values[32:]
    mine = iota((16, rows), 0) == (place & 15)
    out_ref[...] = jnp.sum(jnp.where(mine, values, 0.0), axis=0)


VMEM = pl.BlockSpec(memory_space=pltpu.VMEM)
HBM = pl.BlockSpec(memory_space=pltpu.HBM)
PARAMS = pltpu.CompilerParams(vmem_limit_bytes=40 * 2**20)


def exchange(array):
    return lax.all_to_all(array, AXES, split_axis=0, concat_axis=0, tiled=True)


def local(embeddings, worker, label):
    rows, width = embeddings.shape
    devices = lax.axis_size("shard") * lax.axis_size("grp")
    shape = jax.ShapeDtypeStruct
    packed = (devices * 8, width * 3 // 2)
    in_hbm = [pltpu.with_memory_space_constraint(x, pltpu.HBM) for x in (worker, label, embeddings)]
    outgoing, place = pl.pallas_call(
        pack_kernel,
        out_shape=(shape(packed, BF16), shape((1, rows), jnp.int32)),
        in_specs=[HBM] * 3,
        out_specs=(VMEM, VMEM),
        scratch_shapes=[
            pltpu.VMEM((rows,), jnp.int32),
            pltpu.VMEM((rows,), jnp.int32),
            pltpu.VMEM((rows, width), BF16),
            pltpu.SemaphoreType.DMA((5,)),
        ],
        compiler_params=PARAMS,
        name="pack",
    )(*in_hbm)
    incoming = exchange(outgoing.reshape(devices, 8, packed[1])).reshape(packed)
    found = pl.pallas_call(
        score_kernel,
        out_shape=shape((devices, 128), F32),
        in_specs=[VMEM],
        out_specs=VMEM,
        scratch_shapes=[pltpu.VMEM((SUB, devices * PER_LABEL, width), BF16)],
        compiler_params=PARAMS,
        name="score",
    )(incoming)
    returned = exchange(found.reshape(devices, 1, 128)).reshape(devices, 128)
    return pl.pallas_call(
        unpack_kernel,
        out_shape=shape((rows,), F32),
        in_specs=[VMEM] * 2,
        out_specs=VMEM,
        compiler_params=PARAMS,
        name="unpack",
    )(place, returned)


def solution(mesh):
    return jax.shard_map(
        local,
        mesh=mesh,
        in_specs=(P(AXES, None), P(AXES), P(AXES)),
        out_specs=P(AXES),
        check_vma=False,
    )
```

```python
import functools

import jax
import jax.numpy as jnp
from jax import lax
from jax.experimental import pallas as pl
from jax.experimental.pallas import tpu as pltpu
from jax.sharding import PartitionSpec as P

SUB = 2
AXES = ("shard", "grp")
PER_LABEL = 6
WHOLE = 4
LATE = 2
BLOCK = 256
MARK = 2.0
BF16 = jnp.bfloat16
F32 = jnp.float32


def one_hot(flags):
    return jnp.where(flags, 1.0, 0.0).astype(BF16)


def dot(a, b):
    return jnp.dot(a, b, preferred_element_type=F32)


def dot_rows(a, b):
    return lax.dot_general(a, b, (((1,), (1,)), ((), ())), preferred_element_type=F32)


def iota(shape, dim):
    return lax.broadcasted_iota(jnp.int32, shape, dim)


def small(index):
    return index.astype(F32).astype(BF16)


def merged_rows(a, b, part, swap=0):
    rows, width = a.shape
    first = small((iota((1, 16, width), 1) ^ swap * part) & (2 * part - 1)) < part
    a, b = a.reshape(rows // 16, 16, width), b.reshape(rows // 16, 16, width)
    return jnp.where(first, a, b).reshape(rows, width)


def turned(x):
    rows, width = x.shape
    return pltpu.roll(x.reshape(rows // 8, 8, width), 4, 1).reshape(rows, width)


def upper_half():
    return (lax.axis_index(AXES) >= lax.axis_size(AXES) // 2).astype(jnp.int32)


def pack_kernel(worker_hbm, label_hbm, emb_hbm, out_ref, place_ref, worker_ref, label_ref, emb, arrived):
    rows, width = emb.shape
    half = width // 2
    clusters = out_ref.shape[0] // 4
    pairs = clusters // 4
    fetches = [
        pltpu.make_async_copy(worker_hbm, worker_ref, arrived.at[0]),
        pltpu.make_async_copy(label_hbm, label_ref, arrived.at[1]),
    ]
    bands = [(0, 256), (256, 256), (512, 256)]
    for i, (start, size) in enumerate(bands):
        at = pl.ds(start, size)
        fetches.append(pltpu.make_async_copy(emb_hbm.at[at], emb.at[at], arrived.at[2 + i]))
    for fetch in fetches[:3]:
        fetch.start()
    before = one_hot(iota((BLOCK, BLOCK), 0) < iota((BLOCK, BLOCK), 1))
    ones = jnp.ones((BLOCK, 128), BF16)
    line = small(iota((BLOCK, rows), 0))
    for fetch in fetches[3:]:
        fetch.start()
    fetches[0].wait()
    fetches[1].wait()
    worker = worker_ref[...].reshape(1, rows)
    label = label_ref[...].reshape(1, rows)
    side = label ^ upper_half()
    cluster = worker * SUB + side

    member = iota((clusters, rows), 0) == cluster
    member_hot = one_hot(member)
    count = jnp.zeros((clusters, 128), F32)
    earlier = []
    for part in range(0, rows, BLOCK):
        these = member_hot[:, part : part + BLOCK]
        inside = dot(these, before)
        earlier += [inside[:, k : k + 128] + count for k in range(0, BLOCK, 128)]
        count = count + dot(these, ones)
    earlier = jnp.concatenate(earlier, axis=1)
    rank = jnp.sum(jnp.where(member, earlier, 0.0), axis=0, keepdims=True).astype(jnp.int32)
    place_ref[...] = worker * 16 + label * PER_LABEL + rank
    total = count.astype(BF16)
    whole_row = jnp.where(rank < WHOLE, cluster * WHOLE + rank, -1)
    late_row = (worker & (pairs - 1)) * 8 + side * LATE + rank - WHOLE
    upper = (worker >= pairs).astype(jnp.int32)
    left_row = jnp.where(rank < WHOLE, -1, late_row + upper * 4)
    right_row = jnp.where(rank < WHOLE, -1, late_row + (1 - upper) * 4)
    def chosen(block, target):
        inside = target - block * BLOCK
        inside = jnp.where((inside >= 0) & (inside < BLOCK), inside, -1)
        return jnp.where(line == small(inside), jnp.ones((), BF16), jnp.zeros((), BF16))

    lane = iota((1, 128), 1)

    def filled(spread, counts):
        each = 128 // len(counts)
        merged = counts[0]
        for b in range(1, len(counts)):
            merged = jnp.where(small(lane) < small(jnp.full_like(lane, b * each)), merged, counts[b])
        return dot(one_hot(spread), merged)

    def empty(block, blocks, filled, slot):
        return jnp.where((lane == block * (128 // blocks)) & (filled <= slot.astype(F32)), MARK, 0.0)

    late_blocks = range(pairs * 8 // BLOCK)
    jobs = [(block, target, k * half, half) for block in late_blocks for k, target in enumerate((left_row, right_row))]
    hot = [chosen(block, target) for block, target, _, _ in jobs]
    sums = [0.0] * len(jobs)
    for i, (start, size) in enumerate(bands):
        fetches[2 + i].wait()
        for n, (_, _, column, columns) in enumerate(jobs):
            part = dot(hot[n][:, start : start + size], emb[start : start + size, column : column + columns])
            sums[n] = part if i == 0 else sums[n] + part

    r, c = iota((BLOCK, 128), 0), iota((BLOCK, 128), 1)
    blocks = pairs * 8 // BLOCK
    per_block = BLOCK // 8 * SUB
    spread = c == (r >> 2 & 1) * per_block + (r >> 3) * SUB + (r >> 1 & 1)
    counts = [
        [total[at + block * per_block :][:per_block] for at in (0, clusters // 2)]
        for block in range(blocks)
    ]
    late_filled = filled(spread, [jnp.concatenate(x, axis=0) for x in counts])
    late_slot = WHOLE + (r & 1)
    for block in range(blocks):
        left, right = sums[2 * block], sums[2 * block + 1]
        left_sum = jnp.broadcast_to(jnp.sum(left * left, axis=1, keepdims=True), (BLOCK, 128))
        right_sum = jnp.broadcast_to(jnp.sum(right * right, axis=1, keepdims=True), (BLOCK, 128))
        left_scale = lax.rsqrt(left_sum + turned(right_sum) + 1e-06)[:, :1]
        right_scale = lax.rsqrt(right_sum + turned(left_sum) + 1e-06)[:, :1]
        mark = empty(block, blocks, late_filled, late_slot)
        left = left * left_scale
        left = jnp.concatenate([left[:, :128] + mark, left[:, 128:]], axis=1).astype(BF16)
        right = (right * right_scale).astype(BF16)
        out_ref[pl.ds(block * BLOCK, BLOCK), width:] = merged_rows(left, right, 4)
        out_ref[pl.ds((block + pairs * 8 // BLOCK) * BLOCK, BLOCK), width:] = merged_rows(right, left, 4)
    r, c = iota((BLOCK, BLOCK // WHOLE), 0), iota((BLOCK, BLOCK // WHOLE), 1)
    blocks = clusters * WHOLE // BLOCK
    counts = [total[block * BLOCK // WHOLE :][: BLOCK // WHOLE] for block in range(blocks)]
    whole_filled = filled(c == r >> 2, counts)
    whole_slot = iota((BLOCK, 128), 0) & 3
    for block in range(blocks):
        at = pl.ds(block * BLOCK, BLOCK)
        values = dot(chosen(block, whole_row), emb[...])
        values = values * lax.rsqrt(jnp.sum(values * values, axis=1, keepdims=True) + 1e-06)
        mark = empty(block, blocks, whole_filled, whole_slot)
        out_ref[at, :128] = (values[:, :128] + mark).astype(BF16)
        out_ref[at, 128:width] = values[:, 128:].astype(BF16)


def score_kernel(in_ref, out_ref, members):
    rows = in_ref.shape[0]
    devices = rows // 8
    count, width = members.shape[1:]
    half = width // 2
    wholes = devices * WHOLE

    swap = upper_half()
    lates = wholes // 2
    quarters = [in_ref[k * lates : (k + 1) * lates, width:] for k in range(4)]
    r, c = iota((BLOCK, BLOCK), 0), iota((BLOCK, BLOCK), 1)
    itself = jnp.where(r == c, -8.0, 0.0)
    sub, lane = iota((8, 128), 0), iota((8, 128), 1)
    source = (lane & 15) * 8 + sub

    def in_order(best, start, part, owner):
        total = jnp.zeros((8, 128), F32)
        for v in range(part // 16):
            these = jnp.broadcast_to(best[:, start + v * 128 : start + (v + 1) * 128], (8, 128))
            moved = jnp.take_along_axis(these, source, axis=1)
            total = total + jnp.where((lane >> 4) == owner * (part // 16) + v, moved, 0.0)
        return total

    blocks = count // BLOCK
    found, bests = [], []
    for lab in range(SUB):
        for at in range(0, wholes, BLOCK):
            halves = [in_ref[k * wholes + at : k * wholes + at + BLOCK, :width] for k in (lab, 1 - lab)]
            members[lab, at : at + BLOCK, :] = merged_rows(*halves, 4)
        near, far = [
            merged_rows(quarters[k + 2 * lab], quarters[k + 2 - 2 * lab], 2) for k in (0, 1)
        ]
        straight = merged_rows(near, far, 4)
        crossed = turned(merged_rows(far, near, 4).astype(F32)).astype(BF16)
        members[lab, wholes:, :half] = merged_rows(straight, crossed, 4, swap)
        members[lab, wholes:, half:] = merged_rows(crossed, straight, 4, swap)
        parts = [members[lab, pl.ds(i * BLOCK, BLOCK), :] for i in range(blocks)]
        absent = [
            jnp.min(jnp.where(p[:, :128].astype(F32) > MARK - 0.5, -8.0, 0.0), axis=1, keepdims=True)
            for p in parts
        ]
        absent_row = [jnp.broadcast_to(a, (BLOCK, 128)).T[:1] for a in absent]
        down, along = [[] for _ in parts], [[] for _ in parts]
        for j in reversed(range(blocks)):
            stacked = dot_rows(members[lab, : (j + 1) * BLOCK, :], parts[j])
            for i in range(j + 1):
                scores = stacked[i * BLOCK : (i + 1) * BLOCK] + absent[i]
                if i == j:
                    down[j].append(scores + itself)
                else:
                    down[j].append(scores)
                    scores = scores + absent_row[j]
                    along[i] += [scores[:, k : k + 128] for k in range(0, BLOCK, 128)]
        merged = []
        for i in range(blocks):
            best = jnp.max(functools.reduce(jnp.maximum, down[i]), axis=0, keepdims=True)
            if along[i]:
                other = functools.reduce(jnp.maximum, along[i]).T
                best = jnp.maximum(best, jnp.max(other, axis=0, keepdims=True))
            merged.append(jnp.where(best < -2.0, -1.0, best))
        bests.append(jnp.concatenate(merged, axis=1))
    for lab, best in enumerate(bests):
        whole = in_order(best, 0, devices // 2, sub >> 2 ^ lab)
        whole = whole + pltpu.roll(whole, 4, 0)
        late = in_order(best, wholes, devices // 4, (sub >> 2) + ((sub >> 1 & 1) ^ lab) * 2)
        late = late + pltpu.roll(late, 4, 0)
        late = late + pltpu.roll(late, 2, 0)
        found += [whole[:WHOLE], late[:LATE]]
    found.append(jnp.zeros((128 - SUB * PER_LABEL, devices), F32))
    out_ref[...] = jnp.concatenate(found, axis=0).T


def unpack_kernel(place_ref, back_ref, out_ref):
    place = place_ref[...]
    rows = place.shape[1]
    back = back_ref[...]
    devices = back.shape[0]
    back = back.T[:16]
    high = back.astype(BF16)
    rest = back - high.astype(F32)
    middle = rest.astype(BF16)
    low = (rest - middle.astype(F32)).astype(BF16)
    chosen = one_hot(iota((devices, rows), 0) == place >> 4)
    values = dot(jnp.concatenate([high, middle, low], axis=0), chosen)
    values = values[:16] + values[16:32] + values[32:]
    mine = iota((16, rows), 0) == (place & 15)
    out_ref[...] = jnp.sum(jnp.where(mine, values, 0.0), axis=0)


VMEM = pl.BlockSpec(memory_space=pltpu.VMEM)
HBM = pl.BlockSpec(memory_space=pltpu.HBM)
PARAMS = pltpu.CompilerParams(vmem_limit_bytes=40 * 2**20)


def exchange(array):
    return lax.all_to_all(array, AXES, split_axis=0, concat_axis=0, tiled=True)


def local(embeddings, worker, label):
    rows, width = embeddings.shape
    devices = lax.axis_size("shard") * lax.axis_size("grp")
    shape = jax.ShapeDtypeStruct
    packed = (devices * 8, width * 3 // 2)
    in_hbm = [pltpu.with_memory_space_constraint(x, pltpu.HBM) for x in (worker, label, embeddings)]
    outgoing, place = pl.pallas_call(
        pack_kernel,
        out_shape=(shape(packed, BF16), shape((1, rows), jnp.int32)),
        in_specs=[HBM] * 3,
        out_specs=(VMEM, VMEM),
        scratch_shapes=[
            pltpu.VMEM((rows,), jnp.int32),
            pltpu.VMEM((rows,), jnp.int32),
            pltpu.VMEM((rows, width), BF16),
            pltpu.SemaphoreType.DMA((5,)),
        ],
        compiler_params=PARAMS,
        name="pack",
    )(*in_hbm)
    incoming = exchange(outgoing.reshape(devices, 8, packed[1])).reshape(packed)
    found = pl.pallas_call(
        score_kernel,
        out_shape=shape((devices, 128), F32),
        in_specs=[VMEM],
        out_specs=VMEM,
        scratch_shapes=[pltpu.VMEM((SUB, devices * PER_LABEL, width), BF16)],
        compiler_params=PARAMS,
        name="score",
    )(incoming)
    returned = exchange(found.reshape(devices, 1, 128)).reshape(devices, 128)
    return pl.pallas_call(
        unpack_kernel,
        out_shape=shape((rows,), F32),
        in_specs=[VMEM] * 2,
        out_specs=VMEM,
        compiler_params=PARAMS,
        name="unpack",
    )(place, returned)


def solution(mesh):
    return jax.shard_map(
        local,
        mesh=mesh,
        in_specs=(P(AXES, None), P(AXES), P(AXES)),
        out_specs=P(AXES),
        check_vma=False,
    )
```

```python
import functools

import jax
import jax.numpy as jnp
from jax import lax
from jax.experimental import pallas as pl
from jax.experimental.pallas import tpu as pltpu
from jax.sharding import PartitionSpec as P

SUB = 2
AXES = ("shard", "grp")
PER_LABEL = 6
WHOLE = 4
LATE = 2
BLOCK = 256
MARK = 2.0
BF16 = jnp.bfloat16
F32 = jnp.float32


def one_hot(flags):
    return jnp.where(flags, 1.0, 0.0).astype(BF16)


def dot(a, b):
    return jnp.dot(a, b, preferred_element_type=F32)


def dot_rows(a, b):
    return lax.dot_general(a, b, (((1,), (1,)), ((), ())), preferred_element_type=F32)


def iota(shape, dim):
    return lax.broadcasted_iota(jnp.int32, shape, dim)


def small(index):
    return index.astype(F32).astype(BF16)


def merged_rows(a, b, part, swap=0):
    rows, width = a.shape
    first = small((iota((1, 16, width), 1) ^ swap * part) & (2 * part - 1)) < part
    a, b = a.reshape(rows // 16, 16, width), b.reshape(rows // 16, 16, width)
    return jnp.where(first, a, b).reshape(rows, width)


def turned(x):
    rows, width = x.shape
    return pltpu.roll(x.reshape(rows // 8, 8, width), 4, 1).reshape(rows, width)


def upper_half():
    return (lax.axis_index(AXES) >= lax.axis_size(AXES) // 2).astype(jnp.int32)


def pack_kernel(worker_hbm, label_hbm, emb_hbm, out_ref, place_ref, worker_ref, label_ref, emb, arrived):
    rows, width = emb.shape
    half = width // 2
    clusters = out_ref.shape[0] // 4
    pairs = clusters // 4
    fetches = [
        pltpu.make_async_copy(worker_hbm, worker_ref, arrived.at[0]),
        pltpu.make_async_copy(label_hbm, label_ref, arrived.at[1]),
    ]
    bands = [(0, 256), (256, 256), (512, 256)]
    for i, (start, size) in enumerate(bands):
        at = pl.ds(start, size)
        fetches.append(pltpu.make_async_copy(emb_hbm.at[at], emb.at[at], arrived.at[2 + i]))
    for fetch in fetches[:3]:
        fetch.start()
    before = one_hot(iota((BLOCK, BLOCK), 0) < iota((BLOCK, BLOCK), 1))
    ones = jnp.ones((BLOCK, 128), BF16)
    line = small(iota((BLOCK, rows), 0))
    for fetch in fetches[3:]:
        fetch.start()
    fetches[0].wait()
    fetches[1].wait()
    worker = worker_ref[...].reshape(1, rows)
    label = label_ref[...].reshape(1, rows)
    side = label ^ upper_half()
    cluster = worker * SUB + side

    member = iota((clusters, rows), 0) == cluster
    member_hot = one_hot(member)
    count = jnp.zeros((clusters, 128), F32)
    earlier = []
    for part in range(0, rows, BLOCK):
        these = member_hot[:, part : part + BLOCK]
        inside = dot(these, before)
        earlier += [inside[:, k : k + 128] + count for k in range(0, BLOCK, 128)]
        count = count + dot(these, ones)
    earlier = jnp.concatenate(earlier, axis=1)
    rank = jnp.sum(jnp.where(member, earlier, 0.0), axis=0, keepdims=True).astype(jnp.int32)
    place_ref[...] = worker * 16 + label * PER_LABEL + rank
    total = count.astype(BF16)
    whole_row = jnp.where(rank < WHOLE, cluster * WHOLE + rank, -1)
    late_row = (worker & (pairs - 1)) * 8 + side * LATE + rank - WHOLE
    upper = (worker >= pairs).astype(jnp.int32)
    left_row = jnp.where(rank < WHOLE, -1, late_row + upper * 4)
    right_row = jnp.where(rank < WHOLE, -1, late_row + (1 - upper) * 4)
    def chosen(block, target):
        inside = target - block * BLOCK
        inside = jnp.where((inside >= 0) & (inside < BLOCK), inside, -1)
        return jnp.where(line == small(inside), jnp.ones((), BF16), jnp.zeros((), BF16))

    lane = iota((1, 128), 1)

    def filled(spread, counts):
        each = 128 // len(counts)
        merged = counts[0]
        for b in range(1, len(counts)):
            merged = jnp.where(small(lane) < small(jnp.full_like(lane, b * each)), merged, counts[b])
        return dot(one_hot(spread), merged)

    def empty(block, blocks, filled, slot):
        return jnp.where((lane == block * (128 // blocks)) & (filled <= slot.astype(F32)), MARK, 0.0)

    late_blocks = range(pairs * 8 // BLOCK)
    jobs = [(block, target, k * half, half) for block in late_blocks for k, target in enumerate((left_row, right_row))]
    hot = [chosen(block, target) for block, target, _, _ in jobs]
    sums = [0.0] * len(jobs)
    for i, (start, size) in enumerate(bands):
        fetches[2 + i].wait()
        for n, (_, _, column, columns) in enumerate(jobs):
            part = dot(hot[n][:, start : start + size], emb[start : start + size, column : column + columns])
            sums[n] = part if i == 0 else sums[n] + part

    r, c = iota((BLOCK, 128), 0), iota((BLOCK, 128), 1)
    blocks = pairs * 8 // BLOCK
    per_block = BLOCK // 8 * SUB
    spread = c == (r >> 2 & 1) * per_block + (r >> 3) * SUB + (r >> 1 & 1)
    counts = [
        [total[at + block * per_block :][:per_block] for at in (0, clusters // 2)]
        for block in range(blocks)
    ]
    late_filled = filled(spread, [jnp.concatenate(x, axis=0) for x in counts])
    late_slot = WHOLE + (r & 1)
    for block in range(blocks):
        left, right = sums[2 * block], sums[2 * block + 1]
        left_sum = jnp.broadcast_to(jnp.sum(left * left, axis=1, keepdims=True), (BLOCK, 128))
        right_sum = jnp.broadcast_to(jnp.sum(right * right, axis=1, keepdims=True), (BLOCK, 128))
        left_scale = lax.rsqrt(left_sum + turned(right_sum) + 1e-06)[:, :1]
        right_scale = lax.rsqrt(right_sum + turned(left_sum) + 1e-06)[:, :1]
        mark = empty(block, blocks, late_filled, late_slot)
        left = left * left_scale
        left = jnp.concatenate([left[:, :128] + mark, left[:, 128:]], axis=1).astype(BF16)
        right = (right * right_scale).astype(BF16)
        out_ref[pl.ds(block * BLOCK, BLOCK), width:] = merged_rows(left, right, 4)
        out_ref[pl.ds((block + pairs * 8 // BLOCK) * BLOCK, BLOCK), width:] = merged_rows(right, left, 4)
    r, c = iota((BLOCK, BLOCK // WHOLE), 0), iota((BLOCK, BLOCK // WHOLE), 1)
    blocks = clusters * WHOLE // BLOCK
    counts = [total[block * BLOCK // WHOLE :][: BLOCK // WHOLE] for block in range(blocks)]
    whole_filled = filled(c == r >> 2, counts)
    whole_slot = iota((BLOCK, 128), 0) & 3
    for block in range(blocks):
        at = pl.ds(block * BLOCK, BLOCK)
        values = dot(chosen(block, whole_row), emb[...])
        values = values * lax.rsqrt(jnp.sum(values * values, axis=1, keepdims=True) + 1e-06)
        mark = empty(block, blocks, whole_filled, whole_slot)
        out_ref[at, :128] = (values[:, :128] + mark).astype(BF16)
        out_ref[at, 128:width] = values[:, 128:].astype(BF16)


def score_kernel(in_ref, out_ref, members):
    rows = in_ref.shape[0]
    devices = rows // 8
    count, width = members.shape[1:]
    half = width // 2
    wholes = devices * WHOLE

    swap = upper_half()
    lates = wholes // 2
    quarters = [in_ref[k * lates : (k + 1) * lates, width:] for k in range(4)]
    r, c = iota((BLOCK, BLOCK), 0), iota((BLOCK, BLOCK), 1)
    itself = jnp.where(r == c, -8.0, 0.0)
    sub, lane = iota((8, 128), 0), iota((8, 128), 1)
    source = (lane & 15) * 8 + sub

    def in_order(best, start, part, owner):
        total = jnp.zeros((8, 128), F32)
        for v in range(part // 16):
            these = jnp.broadcast_to(best[:, start + v * 128 : start + (v + 1) * 128], (8, 128))
            moved = jnp.take_along_axis(these, source, axis=1)
            total = total + jnp.where((lane >> 4) == owner * (part // 16) + v, moved, 0.0)
        return total

    blocks = count // BLOCK
    found = []
    for lab in range(SUB):
        near, far = [
            merged_rows(quarters[k + 2 * lab], quarters[k + 2 - 2 * lab], 2) for k in (0, 1)
        ]
        straight = merged_rows(near, far, 4)
        crossed = turned(merged_rows(far, near, 4).astype(F32)).astype(BF16)
        members[lab, wholes:, :half] = merged_rows(straight, crossed, 4, swap)
        members[lab, wholes:, half:] = merged_rows(crossed, straight, 4, swap)
        for at in range(0, wholes, BLOCK):
            halves = [in_ref[k * wholes + at : k * wholes + at + BLOCK, :width] for k in (lab, 1 - lab)]
            members[lab, at : at + BLOCK, :] = merged_rows(*halves, 4)
        parts = [members[lab, pl.ds(i * BLOCK, BLOCK), :] for i in range(blocks)]
        absent = [
            jnp.min(jnp.where(p[:, :128].astype(F32) > MARK - 0.5, -8.0, 0.0), axis=1, keepdims=True)
            for p in parts
        ]
        absent_row = [jnp.broadcast_to(a, (BLOCK, 128)).T[:1] for a in absent]
        down, along = [[] for _ in parts], [[] for _ in parts]
        for j in reversed(range(blocks)):
            stacked = dot_rows(members[lab, : (j + 1) * BLOCK, :], parts[j])
            for i in range(j + 1):
                scores = stacked[i * BLOCK : (i + 1) * BLOCK] + absent[i]
                if i == j:
                    down[j].append(scores + itself)
                else:
                    down[j].append(scores)
                    scores = scores + absent_row[j]
                    along[i] += [scores[:, k : k + 128] for k in range(0, BLOCK, 128)]
        merged = []
        for i in range(blocks):
            best = jnp.max(functools.reduce(jnp.maximum, down[i]), axis=0, keepdims=True)
            if along[i]:
                other = functools.reduce(jnp.maximum, along[i]).T
                best = jnp.maximum(best, jnp.max(other, axis=0, keepdims=True))
            merged.append(jnp.where(best < -2.0, -1.0, best))
        best = jnp.concatenate(merged, axis=1)
        whole = in_order(best, 0, devices // 2, sub >> 2 ^ lab)
        whole = whole + pltpu.roll(whole, 4, 0)
        late = in_order(best, wholes, devices // 4, (sub >> 2) + ((sub >> 1 & 1) ^ lab) * 2)
        late = late + pltpu.roll(late, 4, 0)
        late = late + pltpu.roll(late, 2, 0)
        found += [whole[:WHOLE], late[:LATE]]
    found.append(jnp.zeros((128 - SUB * PER_LABEL, devices), F32))
    out_ref[...] = jnp.concatenate(found, axis=0).T


def unpack_kernel(place_ref, back_ref, out_ref):
    place = place_ref[...]
    rows = place.shape[1]
    back = back_ref[...]
    devices = back.shape[0]
    back = back.T[:16]
    high = back.astype(BF16)
    rest = back - high.astype(F32)
    middle = rest.astype(BF16)
    low = (rest - middle.astype(F32)).astype(BF16)
    chosen = one_hot(iota((devices, rows), 0) == place >> 4)
    values = dot(jnp.concatenate([high, middle, low], axis=0), chosen)
    values = values[:16] + values[16:32] + values[32:]
    mine = iota((16, rows), 0) == (place & 15)
    out_ref[...] = jnp.sum(jnp.where(mine, values, 0.0), axis=0)


VMEM = pl.BlockSpec(memory_space=pltpu.VMEM)
HBM = pl.BlockSpec(memory_space=pltpu.HBM)
PARAMS = pltpu.CompilerParams(vmem_limit_bytes=40 * 2**20)


def exchange(array):
    return lax.all_to_all(array, AXES, split_axis=0, concat_axis=0, tiled=True)


def local(embeddings, worker, label):
    rows, width = embeddings.shape
    devices = lax.axis_size("shard") * lax.axis_size("grp")
    shape = jax.ShapeDtypeStruct
    packed = (devices * 8, width * 3 // 2)
    in_hbm = [pltpu.with_memory_space_constraint(x, pltpu.HBM) for x in (worker, label, embeddings)]
    outgoing, place = pl.pallas_call(
        pack_kernel,
        out_shape=(shape(packed, BF16), shape((1, rows), jnp.int32)),
        in_specs=[HBM] * 3,
        out_specs=(VMEM, VMEM),
        scratch_shapes=[
            pltpu.VMEM((rows,), jnp.int32),
            pltpu.VMEM((rows,), jnp.int32),
            pltpu.VMEM((rows, width), BF16),
            pltpu.SemaphoreType.DMA((5,)),
        ],
        compiler_params=PARAMS,
        name="pack",
    )(*in_hbm)
    incoming = exchange(outgoing.reshape(devices, 8, packed[1])).reshape(packed)
    found = pl.pallas_call(
        score_kernel,
        out_shape=shape((devices, 128), F32),
        in_specs=[VMEM],
        out_specs=VMEM,
        scratch_shapes=[pltpu.VMEM((SUB, devices * PER_LABEL, width), BF16)],
        compiler_params=PARAMS,
        name="score",
    )(incoming)
    returned = exchange(found.reshape(devices, 1, 128)).reshape(devices, 128)
    return pl.pallas_call(
        unpack_kernel,
        out_shape=shape((rows,), F32),
        in_specs=[VMEM] * 2,
        out_specs=VMEM,
        compiler_params=PARAMS,
        name="unpack",
    )(place, returned)


def solution(mesh):
    return jax.shard_map(
        local,
        mesh=mesh,
        in_specs=(P(AXES, None), P(AXES), P(AXES)),
        out_specs=P(AXES),
        check_vma=False,
    )
```
